256 devices in a mesh: section: 8 (over z_lo, x), expert: 8 (over z_hi, core), dp: 4 (over y).
Axes of the slice: x: 4, y: 4, z: 8 (z_hi: 4, z_lo: 2; z = z_hi * 2 + z_lo), core: 2. Of those that a mesh axis runs over, the one named last changes fastest.
Arguments:
- layer_inputs: bfloat16 [4096, 3072], P(('expert', 'dp')), may hold values from -6 to 6
- out_grad: bfloat16 [4096, 3072], P(('expert', 'dp')), may hold values from -6 to 6
- routes: int32 [4096, 2], P(('expert', 'dp')), may hold values from 0 to 7, all different within a row; in each aligned block of 64 rows (0 to 63, 64 to 127, ...) at most 24 rows name the same one
- gates: float32 [4096, 2], P(('expert', 'dp')), may hold values from 0.2 to 1
- w_in: bfloat16 [8, 3072, 8192], P('expert', 'dp', 'section'), may hold values from -0.109375 to 0.109375
- w_out: bfloat16 [8, 8192, 3072], P('expert', 'section', 'dp'), may hold values from -0.0625 to 0.0625
Outputs:
- in_grads: bfloat16 [4096, 3072], P(('expert', 'dp'))
- grad_w_in: bfloat16 [8, 3072, 8192], P('expert', 'dp', 'section')
- grad_w_out: bfloat16 [8, 8192, 3072], P('expert', 'section', 'dp')
The draws below stay inside these ranges and needn't reach their ends.
Inputs may be any that keep to these rules, and one draw needn't show every extreme that they name: `routes`: in each aligned block of 64 rows of tokens no expert is named more than 24 times.
All inputs are finite; a program needn't handle non-finite values.
Results may differ from the reference program's by a relative error of at most 0.02.
Values may be sent and summed in bfloat16 or wider, within the bound.
A program may use at most 128 MiB of HBM per device.

```python
import math
import jax
import jax.numpy as jnp
import numpy as np
from jax import lax

D = 3072
FF = 8192
ROWS = 64
MICRO = 2
TOK_DEV = 128
TOKENS = 4096
EXPERTS = 8
CAP = 24
N_EXPERT = 8
N_DP = 4


def shard_levels(rng, extent, pieces, least, largest):
    def one(dim, shards_of):
        draws = jax.random.uniform(jax.random.fold_in(jax.random.fold_in(rng, 6), dim), (shards_of,), jnp.float32, least / len(pieces), largest / len(pieces))
        return jnp.repeat(jnp.exp(draws), extent[dim] // shards_of).reshape((-1,) + (1,) * (len(extent) - dim - 1))

    factor_of = one(*pieces[0])
    for cut in pieces[1:]:
        factor_of = factor_of * one(*cut)
    return factor_of


def assign_block(key, own, number, rows, count, top, bound, skew):
    order = jax.random.permutation(key, count)
    crowded, common = shares(count, rows * top, bound, skew, True), shares(count, rows * top, bound, skew, False)
    places = jnp.arange(count)

    def named(lengths, turn):
        used = int((lengths > 0).sum())
        fixed = max(1, used // 4)
        passed = fixed + (places - fixed + turn * (used - fixed)) % max(1, count - fixed)
        return jnp.zeros((count,), jnp.int32).at[order[jnp.where(places < fixed, places, passed)]].set(jnp.asarray(lengths, jnp.int32))

    lengths = jnp.where(number % 4 == 0, named(crowded, number // 4), named(common, number - number // 4 - 1))
    mixed = jax.random.permutation(jax.random.fold_in(own, 3), count)
    source_of, taker = mixed[0:count // 2 * 2:2], mixed[1:count // 2 * 2:2]
    margin = jnp.minimum(lengths[source_of] - 1, bound - lengths[taker]) // 2
    margin = jnp.where((source_of == order[0]) | (taker == order[0]) | (lengths[taker] == 0), 0, jnp.maximum(margin, 0))
    passed = jax.random.randint(jax.random.fold_in(own, 4), (count // 2,), 0, 1 << 20) % (margin + 1)
    lengths = lengths.at[source_of].add(-passed).at[taker].add(passed)
    labels = jnp.searchsorted(jnp.cumsum(lengths), jnp.arange(rows * top), side="right").astype(jnp.int32)
    table = labels.reshape(top, rows).T
    table = table[jax.random.permutation(jax.random.fold_in(own, 1), rows)]
    turn = jax.random.randint(jax.random.fold_in(own, 2), (rows, 1), 0, top)
    return jnp.take_along_axis(table, (jnp.arange(top)[None, :] + turn) % top, axis=1)


def shares(number_of, total, bound, skew, full):
    portions = [(1 << 20) // math.isqrt(rank ** skew) + 1 for rank in range(1, number_of + 1)]
    largest = bound if full else min(bound, max(-(-total // number_of), total * portions[0] // sum(portions)))
    least = 1 if total - largest >= number_of - 1 else 0
    given, rest = [largest] + [least] * (number_of - 1), total - largest - least * (number_of - 1)
    while rest > 0:
        free = [i for i in range(1, number_of) if given[i] < largest] or [i for i in range(1, number_of) if given[i] < bound]
        mass, remaining = sum([portions[i] for i in free]), rest
        for i in free:
            extra = min(bound - given[i], max(1, remaining * portions[i] // mass), rest)
            given[i] = given[i] + extra
            rest = rest - extra
    return np.array(given)


def centred(stream_key, extent, deviation, reach, split=(), held_as=jnp.bfloat16):
    factor_of = shard_levels(stream_key, extent, split, -0.22, 0.18) if split else 1.0
    array = jax.random.normal(stream_key, extent, jnp.float32) * deviation * factor_of
    return jnp.minimum(jnp.maximum(array, -reach), reach).astype(held_as)


def setup_inputs(seed: int = 0) -> dict:
    streams_of = jax.random.split(jax.random.key(seed), 7)
    layer_inputs = centred(streams_of[0], (TOKENS, D), 1.0, 6.0, ((0, 32),))
    out_grad = centred(streams_of[1], (TOKENS, D), 1.0, 6.0, ((0, 32),))
    routes_keys = jax.random.split(jax.random.fold_in(streams_of[2], 1), TOKENS // ROWS)
    routes_turns = jax.random.permutation(jax.random.fold_in(streams_of[2], 3), TOKENS // ROWS)
    routes = jax.vmap(lambda own, number: assign_block(jax.random.fold_in(streams_of[2], 2), own, number, ROWS, EXPERTS, 2, CAP, 2))(routes_keys, routes_turns).reshape((TOKENS, 2))
    gates = jnp.clip(0.2 + 0.8 * jax.random.uniform(streams_of[3], (TOKENS, 2), jnp.float32) ** shard_levels(streams_of[3], (TOKENS, 2), ((0, 32),), -0.2, 0.2), 0.2, 1.0)
    w_in = centred(streams_of[4], (EXPERTS, D, FF), D ** -0.5, 0.109375, ((0, 8), (1, 4), (2, 8)))
    w_out = centred(streams_of[5], (EXPERTS, FF, D), FF ** -0.5, 0.0625, ((0, 8), (1, 8), (2, 4)))
    return dict(layer_inputs=layer_inputs, out_grad=out_grad, routes=routes, gates=gates, w_in=w_in, w_out=w_out)


def silu_slope(preact):
    sigmoid_val = jax.nn.sigmoid(preact)
    return sigmoid_val * (1.0 + preact * (1.0 - sigmoid_val))


def expert_pass(token_rows, grad_rows, w_in_local, w_out_local):
    preact = jnp.dot(token_rows, w_in_local, preferred_element_type=jnp.float32)
    hidden = jax.nn.silu(preact).astype(jnp.bfloat16)
    hidden_grad = lax.dot_general(grad_rows, w_out_local, (((1,), (1,)), ((), ())), preferred_element_type=jnp.float32)
    preact_grad = (hidden_grad * silu_slope(preact)).astype(jnp.bfloat16)
    back = lax.dot_general(preact_grad, w_in_local, (((1,), (1,)), ((), ())), preferred_element_type=jnp.float32).astype(jnp.bfloat16)
    return back, hidden, preact_grad


def rounded_wide(value):
    narrow = lax.optimization_barrier(value.astype(jnp.bfloat16))
    return narrow.astype(jnp.float32)


def reference(layer_inputs, out_grad, routes, gates, w_in, w_out):
    total = 2 * TOKENS
    limit = CAP * MICRO * N_EXPERT
    upstream_wide = out_grad.astype(jnp.float32)
    scaled = (gates[:, :, None] * upstream_wide[:, None, :]).astype(jnp.bfloat16)
    scaled_flat = scaled.reshape(total, D)
    flat_routes = routes.reshape(-1)
    group_of = ((jnp.arange(total, dtype=jnp.int32) // 2) // TOK_DEV) % N_DP

    def one_expert(expert_id):
        w_in_here = w_in[expert_id]
        w_out_here = w_out[expert_id]
        grad_one = jnp.zeros((D, FF), jnp.float32)
        grad_two = jnp.zeros((FF, D), jnp.float32)
        backs = []
        places = []
        for group in range(N_DP):
            picked = (flat_routes == expert_id) & (group_of == group)
            position = jnp.nonzero(picked, size=limit, fill_value=total)[0].astype(jnp.int32)
            is_used = position < total
            clipped = jnp.minimum(position, total - 1).astype(jnp.int32)
            token_rows = jnp.where(is_used[:, None], layer_inputs[clipped // 2], jnp.zeros((), jnp.bfloat16)).astype(jnp.bfloat16)
            grad_rows = jnp.where(is_used[:, None], scaled_flat[clipped], jnp.zeros((), jnp.bfloat16)).astype(jnp.bfloat16)
            back, hidden, preact_grad = expert_pass(token_rows, grad_rows, w_in_here, w_out_here)
            part_one = lax.dot_general(token_rows, preact_grad, (((0,), (0,)), ((), ())), preferred_element_type=jnp.float32)
            part_two = lax.dot_general(hidden, grad_rows, (((0,), (0,)), ((), ())), preferred_element_type=jnp.float32)
            grad_one = grad_one + rounded_wide(part_one)
            grad_two = grad_two + rounded_wide(part_two)
            backs.append(jnp.where(is_used[:, None], back.astype(jnp.float32), jnp.zeros((), jnp.float32)))
            places.append(clipped)
        return jnp.stack(backs), jnp.stack(places), grad_one.astype(jnp.bfloat16), grad_two.astype(jnp.bfloat16)

    backs, places, grad_one, grad_two = lax.map(one_expert, jnp.arange(EXPERTS, dtype=jnp.int32))
    contrib = jnp.zeros((total, D), jnp.float32).at[places.reshape(-1)].add(backs.reshape(-1, D))
    contrib = contrib.reshape(TOKENS, 2, D)
    in_grads = ((upstream_wide + contrib[:, 0]) + contrib[:, 1]).astype(jnp.bfloat16)
    return in_grads, grad_one, grad_two
```

```python
import jax
import jax.numpy as jnp
from jax import lax
from jax.experimental import pallas as pl
from jax.experimental.pallas import tpu as pltpu
from jax.sharding import PartitionSpec as P

MESH = pl.DeviceIdType.MESH
F32 = jnp.float32
BF16 = jnp.bfloat16

ROWS = 64
NX = 4
NY = 4
NZ = 4
SLOTS = 48
D_LOC = 768
HALF = D_LOC // 2
F_LOC = 1024
TILE = 256

FROM_Z = (0, 1, 3, 2)
A2A, BZ, B_OWN, B_OTHER, B_FWD = 0, 2, 3, 5, 7
R_FAR, R_NEAR, R_SUM = 9, 11, 13
G_OWN, G_FWD = 15, 17
PART = 19
S_FAR, S_NEAR, S_SUM, S_Z = 38, 40, 42, 44
HOME = 45
COPIES = 47
O_Z, O_OWN, O_OTHER, O_FWD = 0, 1, 3, 5
OUT_COPIES = 7
PLAN = (
    "s00", "s01", "a00", "b00", "s10", "c00", "a01", "b01", "s11", "d00", "c01", "a10", "b10", "s20",
    "s21", "e00", "d01", "c10", "a11", "b11", "e01", "d10", "c11", "s30", "s31", "a20", "b20", "f0",
    "e10", "d11", "c20", "a21", "b21", "g0", "e11", "d20", "c21", "a30", "b30", "f1", "e20", "d21",
    "c30", "a31", "b31", "g1", "h0", "e21", "d30", "c31", "f2", "e30", "d31", "g2", "h1", "i0",
    "e31", "f3", "i1", "j0", "h2", "g3", "o0", "o1", "o2", "o3", "j1", "l0", "i2", "h3",
    "l1", "j2", "u0", "i3", "l2", "u1", "j3", "u2", "l3", "q0", "w0", "q1", "w1", "q2",
    "w2", "q3", "v0", "v1", "v2", "v3", "x0", "x1", "x2", "x3", "w3",
)


def kernel(
    x_ref,
    up_ref,
    routes_ref,
    gates_ref,
    w_in_ref,
    w_out_ref,
    ing_ref,
    gin_ref,
    gout_ref,
    xg,
    ps,
    r1,
    r2,
    hp,
    bk,
    q1,
    q2,
    q3,
    rb,
    ret,
    ssem,
    rsem,
    osend,
    orecv,
    lsem,
    w_in,
    w_out,
    gin,
    gout,
    ing,
    acc,
    xs,
    us,
    send,
    comb,
):
    section = lax.axis_index("section")
    expert = lax.axis_index("expert")
    y = lax.axis_index("dp")
    x, c = lax.rem(section, NX), section // NX
    zh, core = expert // 2, lax.rem(expert, 2)

    def around(value, n=4):
        return lax.rem(value + 2 * n, n)

    x_dev = (
        {"section": c * NX + around(x + 1)},
        {"section": c * NX + around(x - 1)},
    )
    z_dev = {"section": (1 - c) * NX + x}
    y_dev = ({"dp": around(y + 1)}, {"dp": around(y - 1)})
    y_to = around(y - x)
    y_from = around(y + x)
    to_cols = pl.ds(pl.multiple_of(y_to * D_LOC + c * HALF, 128), HALF)
    mine = pl.ds(pl.multiple_of(c * HALF, 128), HALF)
    other = pl.ds(pl.multiple_of((1 - c) * HALF, 128), HALF)

    def load(n):
        src, dst = (
            (w_in_ref, w_in),
            (w_out_ref, w_out),
            (x_ref.at[:, to_cols], xs),
            (up_ref.at[:, to_cols], us),
        )[n]
        return pltpu.make_async_copy(src, dst, lsem.at[n])

    for n in (2, 3, 0, 1):
        load(n).start()
    stores = []

    def store(src, dst, rows, n):
        copy = pltpu.make_async_copy(src.at[rows], dst.at[rows], lsem.at[4 + n])
        copy.start()
        stores.append(copy)

    barrier = pltpu.get_barrier_semaphore()
    for dev in x_dev + y_dev + (z_dev,):
        pl.semaphore_signal(barrier, inc=1, device_id=dev, device_id_type=MESH)
    for e in range(2 * NZ):
        for yy in (y_to, y_from):

            @pl.when(jnp.logical_or(x != 0, expert != e))
            def _(e=e, yy=yy):
                pl.semaphore_signal(
                    barrier,
                    inc=1,
                    device_id={"expert": jnp.int32(e), "dp": yy},
                    device_id_type=MESH,
                )

    tokens, count = us.shape[0], 2 * NZ * SLOTS
    place = lax.broadcasted_iota(jnp.int32, (tokens, count), 1)
    expert_of = sum((place >= SLOTS * e).astype(jnp.int32) for e in range(1, 2 * NZ))
    token = lax.broadcasted_iota(jnp.int32, (tokens, count), 0)
    micro_start = jnp.where(token >= ROWS, SLOTS // 2, 0)
    is_first = routes_ref[:, 0:1] == expert_of
    is_second = routes_ref[:, 1:2] == expert_of
    named = jnp.logical_or(is_first, is_second)
    row = lax.broadcasted_iota(jnp.int32, (tokens, tokens), 0)
    col = lax.broadcasted_iota(jnp.int32, (tokens, tokens), 1)
    earlier = jnp.logical_and(col < row, col >= jnp.where(row >= ROWS, ROWS, 0))

    def ones(mask):
        return jnp.where(mask, 1.0, 0.0).astype(BF16)

    before = jnp.dot(ones(earlier), ones(named), preferred_element_type=F32)
    slot = (place - SLOTS * expert_of - micro_start).astype(F32)
    taken = jnp.logical_and(named, before == slot)
    comb[...] = ones(taken)

    def picked(mask, rows):
        return lax.dot_general(
            ones(mask), rows, (((0,), (0,)), ((), ())), preferred_element_type=F32
        )

    load(2).wait()
    send[0] = picked(taken, xs[...]).astype(BF16).reshape(2 * NZ, SLOTS, HALF)
    load(3).wait()
    wide = us[...].astype(F32)
    send[1] = (
        picked(jnp.logical_and(taken, is_first), (gates_ref[:, 0:1] * wide).astype(BF16))
        + picked(jnp.logical_and(taken, is_second), (gates_ref[:, 1:2] * wide).astype(BF16))
    ).astype(BF16).reshape(2 * NZ, SLOTS, HALF)

    pl.semaphore_wait(barrier, jnp.where(x == 0, 19, 21))

    sent = []

    def remote(src, dst, k, j, dev, rj=None):
        return pltpu.make_async_remote_copy(
            src_ref=src,
            dst_ref=dst,
            send_sem=ssem.at[k, j],
            recv_sem=rsem.at[k, j if rj is None else rj],
            device_id=dev,
            device_id_type=MESH,
        )

    def push(src, dst, k, j, dev, rj=None):
        copy = remote(src, dst, k, j, dev, rj)
        copy.start()
        sent.append(copy)

    def arrived(dst, k, j):
        remote(dst, dst, k, j, z_dev).wait_recv()

    def push_expert(src, dst, k, j, e, yy, rj):
        if k != 0:
            push(src, dst, k, j, {"expert": e, "dp": yy}, rj)
            return
        own = jnp.logical_and(x == 0, expert == e)
        copy = remote(src, dst, k, j, {"expert": e, "dp": yy}, rj)
        local = pltpu.make_async_copy(src, dst, rsem.at[k, rj])

        @pl.when(own)
        def _():
            local.start()

        @pl.when(jnp.logical_not(own))
        def _():
            copy.start()

        class Guarded:
            def wait_send(self):
                @pl.when(jnp.logical_not(own))
                def _():
                    copy.wait_send()

        sent.append(Guarded())

    def start_dispatch(k, m):
        zd = around(zh - FROM_Z[k])
        for to_core in range(2):
            e = zd * 2 + to_core
            push_expert(
                send.at[m, e],
                xg.at[m, k, y, core, :, mine],
                k,
                PART * m + A2A + to_core,
                e,
                y_to,
                PART * m + A2A + core,
            )

    def piece(k, m, dx, cols):
        return xg.at[m, k, around(y + x + dx), :, :, cols]

    def share(ref, k, j, dev):
        push(ref, ref, k, j, dev)

    def share_own(k, m):
        for b in range(2):
            arrived(xg.at[m, k, y_from, b, :, mine], k, PART * m + A2A + b)
        share(piece(k, m, 0, mine), k, PART * m + BZ, z_dev)
        for i in range(2):
            share(piece(k, m, 0, mine), k, PART * m + B_OWN + i, x_dev[i])

    def share_other(k, m):
        arrived(piece(k, m, 0, other), k, PART * m + BZ)
        for i in range(2):
            share(piece(k, m, 0, other), k, PART * m + B_OTHER + i, x_dev[i])

    def share_far(k, m):
        arrived(piece(k, m, -1, mine), k, PART * m + B_OWN)
        share(piece(k, m, -1, mine), k, PART * m + B_FWD, x_dev[0])
        arrived(piece(k, m, 1, other), k, PART * m + B_OTHER + 1)
        share(piece(k, m, 1, other), k, PART * m + B_FWD + 1, x_dev[1])

    def project(k, m):
        if k == 0:
            load(m).wait()
        arrived(piece(k, m, 1, mine), k, PART * m + B_OWN + 1)
        arrived(piece(k, m, -1, other), k, PART * m + B_OTHER)
        arrived(piece(k, m, 2, mine), k, PART * m + B_FWD)
        arrived(piece(k, m, 2, other), k, PART * m + B_FWD + 1)

        def body(n, _):
            cols = pl.ds(pl.multiple_of(n * TILE, TILE), TILE)
            rows = xg[m, k].reshape(NY * 2 * SLOTS, D_LOC)
            if m == 0:
                part = jnp.dot(rows, w_in[:, cols], preferred_element_type=F32)
            else:
                part = lax.dot_general(
                    rows, w_out[cols, :], (((1,), (1,)), ((), ())), preferred_element_type=F32
                )
            ps[k, m, :, :, :, cols] = part.astype(BF16).reshape(NY, 2, SLOTS, TILE)
            return 0

        lax.fori_loop(0, F_LOC // TILE, body, 0)
        far, after, before = (around(y + d) for d in (2, 1, -1))
        j = PART * m
        push(ps.at[k, m, far, 0], r1.at[k, m, 0], k, j + R_FAR, y_dev[0])
        push(ps.at[k, m, far, 1], r1.at[k, m, 1], k, j + R_FAR + 1, y_dev[1])
        push(ps.at[k, m, after, 1], r2.at[k, m, 0, 1], k, j + R_NEAR, y_dev[0])
        push(ps.at[k, m, before, 0], r2.at[k, m, 1, 0], k, j + R_NEAR + 1, y_dev[1])

    def pass_sums(k, m):
        for i in range(2):
            arrived(r1.at[k, m, i], k, PART * m + R_FAR + i)
            to = around(y + 1 - 2 * i)
            total = ps[k, m, to, i].astype(F32) + r1[k, m, i].astype(F32)
            ps[k, m, to, i] = total.astype(BF16)
            push(ps.at[k, m, to, i], r2.at[k, m, i, i], k, PART * m + R_SUM + i, y_dev[i])

    def activate(k):
        for m in range(2):
            for i in range(2):
                arrived(r2.at[k, m, i, 1 - i], k, PART * m + R_NEAR + i)
                arrived(r2.at[k, m, i, i], k, PART * m + R_SUM + i)
        for b in range(2):
            pre, grad = (
                ps[k, m, y, b].astype(F32)
                + r2[k, m, 0, b].astype(F32)
                + r2[k, m, 1, b].astype(F32)
                for m in range(2)
            )
            s = jax.nn.sigmoid(pre)
            hp[0, k, y, b] = (pre * s).astype(BF16)
            hp[1, k, y, b] = (grad * (s * (1.0 + pre * (1.0 - s)))).astype(BF16)
        gather_own(k, 1)

    def gather_own(k, m):
        for i in range(2):
            share(hp.at[m, k, y], k, PART * m + G_OWN + i, y_dev[i])

    def gather_far(k, m):
        for i in range(2):
            near = around(y - 1 + 2 * i)
            arrived(hp.at[m, k, near], k, PART * m + G_OWN + i)
            share(hp.at[m, k, near, i], k, PART * m + G_FWD + i, y_dev[i])

    def gathered(k, m):
        for i in range(2):
            arrived(hp.at[m, k, around(y + 2), i], k, PART * m + G_FWD + i)

    def go_back(k):
        gathered(k, 1)

        def body(n, _):
            cols = pl.ds(pl.multiple_of(n * TILE, TILE), TILE)
            part = lax.dot_general(
                hp[1, k].reshape(NY * 2 * SLOTS, F_LOC),
                w_in[cols, :],
                (((1,), (1,)), ((), ())),
                preferred_element_type=F32,
            )
            bk[k, :, :, :, cols] = part.astype(BF16).reshape(NY, 2, SLOTS, TILE)
            return 0

        lax.fori_loop(0, D_LOC // TILE, body, 0)
        far, after, before = (around(y + x + d) for d in (2, 1, -1))
        push(bk.at[k, far, 0], q1.at[k, 0], k, S_FAR, x_dev[0])
        push(bk.at[k, far, 1], q1.at[k, 1], k, S_FAR + 1, x_dev[1])
        push(bk.at[k, after, 1], q2.at[k, 0, 1], k, S_NEAR, x_dev[0])
        push(bk.at[k, before, 0], q2.at[k, 1, 0], k, S_NEAR + 1, x_dev[1])

    def back_sums(k):
        for i in range(2):
            arrived(q1.at[k, i], k, S_FAR + i)
            to = around(y + x + 1 - 2 * i)
            total = bk[k, to, i].astype(F32) + q1[k, i].astype(F32)
            bk[k, to, i] = total.astype(BF16)
            push(bk.at[k, to, i], q2.at[k, i, i], k, S_SUM + i, x_dev[i])

    def back_across(k):
        for i in range(2):
            arrived(q2.at[k, i, 1 - i], k, S_NEAR + i)
            arrived(q2.at[k, i, i], k, S_SUM + i)
        for b in range(2):
            total = (
                bk[k, y_from, b].astype(F32) + q2[k, 0, b].astype(F32) + q2[k, 1, b].astype(F32)
            )
            bk[k, y_from, b] = total.astype(BF16)
        push(bk.at[k, y_from, :, :, other], q3.at[k], k, S_Z, z_dev)

    def send_home(k):
        arrived(q3.at[k], k, S_Z)
        rb[k] = (bk[k, y_from, :, :, mine].astype(F32) + q3[k].astype(F32)).astype(BF16)
        zs = around(zh + FROM_Z[k])
        for to_core in range(2):
            push_expert(
                rb.at[k, to_core],
                ret.at[expert],
                k,
                HOME + to_core,
                zs * 2 + to_core,
                y_from,
                HOME + core,
            )

    def weight_in(n):
        rows = pl.ds(n * TILE, TILE)
        gin[rows, :] = lax.dot_general(
            xg[0, :, :, :, :, rows].reshape(NZ * NY * 2 * SLOTS, TILE),
            hp[1].reshape(NZ * NY * 2 * SLOTS, F_LOC),
            (((0,), (0,)), ((), ())),
            preferred_element_type=F32,
        ).astype(BF16)
        store(gin, gin_ref, rows, n)

    def weight_out(n):
        if n == 0:
            for k in range(NZ - 1):
                gathered(k, 0)
        rows = pl.ds(n * TILE, TILE)
        acc[rows, :] = lax.dot_general(
            hp[0, : NZ - 1, :, :, :, rows].reshape((NZ - 1) * NY * 2 * SLOTS, TILE),
            xg[1, : NZ - 1].reshape((NZ - 1) * NY * 2 * SLOTS, D_LOC),
            (((0,), (0,)), ((), ())),
            preferred_element_type=F32,
        )

    def weight_out_last(n):
        if n == 0:
            gathered(NZ - 1, 0)
        rows = pl.ds(n * TILE, TILE)
        part = lax.dot_general(
            hp[0, NZ - 1, :, :, :, rows].reshape(NY * 2 * SLOTS, TILE),
            xg[1, NZ - 1].reshape(NY * 2 * SLOTS, D_LOC),
            (((0,), (0,)), ((), ())),
            preferred_element_type=F32,
        )
        gout[rows, :] = (acc[rows, :] + part).astype(BF16)
        store(gout, gout_ref, rows, 3 + n)

    def out_piece(dx, half):
        start = around(y - x - dx) * D_LOC + half * HALF
        return ing.at[:, pl.ds(pl.multiple_of(start, 128), HALF)]

    def out_copy(ref, j, dev):
        return pltpu.make_async_remote_copy(
            src_ref=ref,
            dst_ref=ref,
            send_sem=osend.at[j],
            recv_sem=orecv.at[j],
            device_id=dev,
            device_id_type=MESH,
        )

    def out_push(ref, j, dev):
        copy = out_copy(ref, j, dev)
        copy.start()
        sent.append(copy)

    def out_arrived(ref, j):
        out_copy(ref, j, z_dev).wait_recv()

    def combine():
        for k in range(NZ):
            for b in range(2):
                arrived(ret.at[around(zh - FROM_Z[k]) * 2 + b], k, HOME + b)
        contrib = jnp.dot(
            comb[...], ret[...].reshape(2 * NZ * SLOTS, HALF), preferred_element_type=F32
        )
        start = y_to * D_LOC + c * HALF
        ing[:, pl.ds(pl.multiple_of(start, 128), HALF)] = (
            us[...].astype(F32) + contrib
        ).astype(BF16)
        out_push(out_piece(0, c), O_Z, z_dev)
        for i in range(2):
            out_push(out_piece(0, c), O_OWN + i, x_dev[i])

    def out_other():
        out_arrived(out_piece(0, 1 - c), O_Z)
        for i in range(2):
            out_push(out_piece(0, 1 - c), O_OTHER + i, x_dev[i])

    def out_far():
        out_arrived(out_piece(-1, c), O_OWN)
        out_push(out_piece(-1, c), O_FWD, x_dev[0])
        out_arrived(out_piece(1, 1 - c), O_OTHER + 1)
        out_push(out_piece(1, 1 - c), O_FWD + 1, x_dev[1])

    def out_end():
        out_arrived(out_piece(1, c), O_OWN + 1)
        out_arrived(out_piece(-1, 1 - c), O_OTHER)
        out_arrived(out_piece(2, c), O_FWD)
        out_arrived(out_piece(2, 1 - c), O_FWD + 1)

    steps = dict(
        a=share_own,
        b=share_other,
        c=share_far,
        d=project,
        e=pass_sums,
        f=activate,
        o=lambda k: gather_own(k, 0),
        g=lambda k: gather_far(k, 1),
        q=lambda k: gather_far(k, 0),
        h=go_back,
        i=back_sums,
        j=back_across,
        l=send_home,
        u=weight_in,
        v=weight_out,
        x=weight_out_last,
        s=start_dispatch,
        w=lambda n: (combine, out_other, out_far, out_end)[n](),
    )
    for word in PLAN:
        steps[word[0]](*(int(n) for n in word[1:]))
    store(ing, ing_ref, pl.ds(0, ing.shape[0]), 7)
    for copy in stores:
        copy.wait()
    for copy in sent:
        copy.wait_send()


def on_device(layer_inputs, out_grad, routes, gates, w_in, w_out):
    tokens = layer_inputs.shape[0]
    vmem = pl.BlockSpec(memory_space=pltpu.VMEM)
    hbm = pl.BlockSpec(memory_space=pl.ANY)
    rows = NY * 2 * SLOTS
    flops = 5 * 2 * NZ * rows * D_LOC * F_LOC
    in_grads, grad_in, grad_out = pl.pallas_call(
        kernel,
        out_shape=(
            jax.ShapeDtypeStruct(layer_inputs.shape, BF16),
            jax.ShapeDtypeStruct((D_LOC, F_LOC), BF16),
            jax.ShapeDtypeStruct((F_LOC, D_LOC), BF16),
        ),
        in_specs=[hbm] * 2 + [vmem] * 2 + [hbm] * 2,
        out_specs=(hbm,) * 3,
        scratch_shapes=[
            pltpu.VMEM((2, NZ, NY, 2, SLOTS, D_LOC), BF16),
            pltpu.VMEM((NZ, 2, NY, 2, SLOTS, F_LOC), BF16),
            pltpu.VMEM((NZ, 2, 2, SLOTS, F_LOC), BF16),
            pltpu.VMEM((NZ, 2, 2, 2, SLOTS, F_LOC), BF16),
            pltpu.VMEM((2, NZ, NY, 2, SLOTS, F_LOC), BF16),
            pltpu.VMEM((NZ, NY, 2, SLOTS, D_LOC), BF16),
            pltpu.VMEM((NZ, 2, SLOTS, D_LOC), BF16),
            pltpu.VMEM((NZ, 2, 2, SLOTS, D_LOC), BF16),
            pltpu.VMEM((NZ, 2, SLOTS, HALF), BF16),
            pltpu.VMEM((NZ, 2, SLOTS, HALF), BF16),
            pltpu.VMEM((2 * NZ, SLOTS, HALF), BF16),
            pltpu.SemaphoreType.DMA((NZ, COPIES)),
            pltpu.SemaphoreType.DMA((NZ, COPIES)),
            pltpu.SemaphoreType.DMA((OUT_COPIES,)),
            pltpu.SemaphoreType.DMA((OUT_COPIES,)),
            pltpu.SemaphoreType.DMA((12,)),
            pltpu.VMEM((D_LOC, F_LOC), BF16),
            pltpu.VMEM((F_LOC, D_LOC), BF16),
            pltpu.VMEM((D_LOC, F_LOC), BF16),
            pltpu.VMEM((F_LOC, D_LOC), BF16),
            pltpu.VMEM(layer_inputs.shape, BF16),
            pltpu.VMEM((F_LOC, D_LOC), F32),
            pltpu.VMEM((tokens, HALF), BF16),
            pltpu.VMEM((tokens, HALF), BF16),
            pltpu.VMEM((2, 2 * NZ, SLOTS, HALF), BF16),
            pltpu.VMEM((tokens, 2 * NZ * SLOTS), BF16),
        ],
        compiler_params=pltpu.CompilerParams(
            collective_id=0, has_side_effects=True, vmem_limit_bytes=56 * 2**20
        ),
        cost_estimate=pl.CostEstimate(flops=flops, bytes_accessed=2**23, transcendentals=0),
    )(layer_inputs, out_grad, routes, gates, w_in[0], w_out[0])
    return (in_grads, grad_in[None], grad_out[None])


def solution(mesh):
    assert dict(mesh.shape) == {"section": 2 * NX, "expert": 2 * NZ, "dp": NY}
    return jax.shard_map(
        on_device,
        mesh=mesh,
        in_specs=(
            P(("expert", "dp"), None),
            P(("expert", "dp"), None),
            P(("expert", "dp"), None),
            P(("expert", "dp"), None),
            P("expert", "dp", "section"),
            P("expert", "section", "dp"),
        ),
        out_specs=(
            P(("expert", "dp"), None),
            P("expert", "dp", "section"),
            P("expert", "section", "dp"),
        ),
        check_vma=False,
    )
```

```python
import jax
import jax.numpy as jnp
from jax import lax
from jax.experimental import pallas as pl
from jax.experimental.pallas import tpu as pltpu
from jax.sharding import PartitionSpec as P

MESH = pl.DeviceIdType.MESH
F32 = jnp.float32
BF16 = jnp.bfloat16

ROWS = 64
NX = 4
NY = 4
NZ = 4
SLOTS = 48
D_LOC = 768
HALF = D_LOC // 2
F_LOC = 1024
TILE = 256

FROM_Z = (0, 1, 3, 2)
A2A, BZ, B_OWN, B_OTHER, B_FWD = 0, 2, 3, 5, 7
R_FAR, R_NEAR, R_SUM = 9, 11, 13
G_OWN, G_FWD = 15, 17
PART = 19
S_FAR, S_NEAR, S_SUM, S_Z = 38, 40, 42, 44
HOME = 45
COPIES = 47
O_Z, O_OWN, O_OTHER, O_FWD = 0, 1, 3, 5
OUT_COPIES = 7
PLAN = (
    "s01", "s00", "s10", "s31", "a01", "s20", "s11", "s30", "a00", "C01", "c01", "a20", "C00", "c00",
    "s21", "d01", "a31", "b20", "d00", "a21", "c20", "b31", "e01", "C20", "b21", "a30", "C31", "e00",
    "c31", "d20", "a10", "c21", "C21", "b30", "a11", "d31", "b11", "d21", "c10", "C30", "b10", "e31",
    "C10", "e20", "C11", "c11", "e21", "d10", "d11", "e10", "c30", "d30", "f2", "e11", "e30", "g2",
    "f1", "f3", "g1", "h2", "f0", "g3", "i2", "h1", "g0", "i1", "o0", "o2", "j2", "h3",
    "j1", "h0", "u2", "l1", "i3", "i0", "o1", "u1", "j3", "l2", "q2", "j0", "u0", "l3",
    "l0", "q1", "o3", "w0", "q0", "w1", "q3", "w2", "v2", "v3", "v0", "x0", "v1", "x1",
    "x2", "x3", "w3",
)


def kernel(
    x_ref,
    up_ref,
    routes_ref,
    gates_ref,
    w_in_ref,
    w_out_ref,
    ing,
    gin,
    gout,
    xg,
    ps,
    r1,
    r2,
    hp,
    bk,
    q1,
    q2,
    q3,
    rb,
    ret,
    ssem,
    rsem,
    osend,
    orecv,
    lsem,
    w_in,
    w_out,
    acc,
    xs,
    us,
    send,
    comb,
    gate,
):
    section = lax.axis_index("section")
    expert = lax.axis_index("expert")
    y = lax.axis_index("dp")
    x, c = lax.rem(section, NX), section // NX
    zh, core = expert // 2, lax.rem(expert, 2)

    def around(value, n=4):
        return lax.rem(value + 2 * n, n)

    x_dev = (
        {"section": c * NX + around(x + 1)},
        {"section": c * NX + around(x - 1)},
    )
    z_dev = {"section": (1 - c) * NX + x}
    y_dev = ({"dp": around(y + 1)}, {"dp": around(y - 1)})
    y_to = around(y - x)
    y_from = around(y + x)
    mine = pl.ds(pl.multiple_of(c * HALF, 128), HALF)
    other = pl.ds(pl.multiple_of((1 - c) * HALF, 128), HALF)

    def load(n):
        src, dst = (
            (w_in_ref, w_in),
            (w_out_ref, w_out),
            (x_ref, xs),
            (up_ref, us),
        )[n]
        return pltpu.make_async_copy(src, dst, lsem.at[n])

    for n in (2, 3, 0, 1):
        load(n).start()
    barrier = pltpu.get_barrier_semaphore()
    for dev in x_dev + y_dev + (z_dev,):
        pl.semaphore_signal(barrier, inc=1, device_id=dev, device_id_type=MESH)
    for k in range(NZ):
        ahead, behind = around(zh + FROM_Z[k]), around(zh - FROM_Z[k])
        pairs = [(behind, around(y - x - k)), (ahead, around(y + x + k))]
        if k > 0:
            pairs += [(ahead, y_from), (behind, y_to)]
        for to_core in range(2):
            for zz, yy in pairs:

                def greet(e=zz * 2 + to_core, yy=yy):
                    pl.semaphore_signal(
                        barrier,
                        inc=1,
                        device_id={"expert": e, "dp": yy},
                        device_id_type=MESH,
                    )

                if k > 0:
                    greet()
                else:
                    pl.when(jnp.logical_or(x != 0, core != to_core))(greet)

    tokens, count = us.shape[0], 2 * NZ * SLOTS
    place = lax.broadcasted_iota(jnp.int32, (count, tokens), 0)
    expert_of, slot = jnp.zeros_like(place), place
    for k in range(NZ):
        for b in range(2):
            start = (2 * k + b) * SLOTS
            here = place >= start
            expert_of = jnp.where(here, around(zh - FROM_Z[k]) * 2 + b, expert_of)
            slot = jnp.where(here, place - start, slot)
    token = lax.broadcasted_iota(jnp.int32, (count, tokens), 1)
    slot = slot - jnp.where(token >= ROWS, SLOTS // 2, 0)
    is_first = routes_ref[0:1, :] == expert_of
    is_second = routes_ref[1:2, :] == expert_of
    named = jnp.logical_or(is_first, is_second)
    row = lax.broadcasted_iota(jnp.int32, (tokens, tokens), 0)
    col = lax.broadcasted_iota(jnp.int32, (tokens, tokens), 1)
    earlier = jnp.logical_and(row < col, row >= jnp.where(col >= ROWS, ROWS, 0))

    def ones(mask):
        return jnp.where(mask, 1.0, 0.0).astype(BF16)

    before = jnp.dot(ones(named), ones(earlier), preferred_element_type=F32)
    taken = jnp.logical_and(named, before == slot.astype(F32))
    comb[0] = ones(taken)
    comb[1] = ones(jnp.logical_and(taken, is_first))
    comb[2] = ones(jnp.logical_and(taken, is_second))
    for i in range(2):
        gate[i] = jnp.broadcast_to(gates_ref[i : i + 1, :], (tokens, tokens)).T
    load(2).wait()
    load(3).wait()

    def pick(k, m):
        rows = pl.ds(2 * k * SLOTS, 2 * SLOTS)
        first = around(y - x - k) * D_LOC
        for half in (0, 1) if k == 0 else (c,):
            cols = pl.ds(pl.multiple_of(first + half * HALF, 128), HALF)
            if m == 0:
                part = jnp.dot(comb[0, rows], xs[:, cols], preferred_element_type=F32)
            else:
                part = 0.0
                wide = us[:, cols].astype(F32)
                for i in range(2):
                    weight = jnp.concatenate([gate[i]] * (HALF // tokens), axis=1)
                    part = part + jnp.dot(
                        comb[1 + i, rows],
                        (weight * wide).astype(BF16),
                        preferred_element_type=F32,
                    )
            place_in = pl.ds(half * HALF, HALF) if k == 0 else mine
            send[m, k, :, :, place_in] = part.astype(BF16).reshape(2, SLOTS, HALF)

    pick(0, 0)
    pl.semaphore_wait(barrier, jnp.where(x == 0, 31, 33))

    sent = []

    def remote(src, dst, k, j, dev, rj=None):
        return pltpu.make_async_remote_copy(
            src_ref=src,
            dst_ref=dst,
            send_sem=ssem.at[k, j],
            recv_sem=rsem.at[k, j if rj is None else rj],
            device_id=dev,
            device_id_type=MESH,
        )

    def push(src, dst, k, j, dev, rj=None):
        copy = remote(src, dst, k, j, dev, rj)
        copy.start()
        sent.append(copy)

    def arrived(dst, k, j):
        remote(dst, dst, k, j, z_dev).wait_recv()

    def push_expert(src, dst, k, j, e, yy, rj):
        if k != 0:
            push(src, dst, k, j, {"expert": e, "dp": yy}, rj)
            return
        own = jnp.logical_and(x == 0, expert == e)
        copy = remote(src, dst, k, j, {"expert": e, "dp": yy}, rj)
        local = pltpu.make_async_copy(src, dst, rsem.at[k, rj])

        @pl.when(own)
        def _():
            local.start()

        @pl.when(jnp.logical_not(own))
        def _():
            copy.start()

        class Guarded:
            def wait_send(self):
                @pl.when(jnp.logical_not(own))
                def _():
                    copy.wait_send()

        sent.append(Guarded())

    def width(k):
        return pl.ds(0, D_LOC) if k == 0 else mine

    def start_dispatch(k, m):
        if (k, m) != (0, 0):
            pick(k, m)
        zd = around(zh - FROM_Z[k])
        for to_core in range(2):
            e = zd * 2 + to_core
            push_expert(
                send.at[m, k, to_core, :, width(k)],
                xg.at[m, k, y, core, :, width(k)],
                k,
                PART * m + A2A + to_core,
                e,
                around(y - x - k),
                PART * m + A2A + core,
            )

    def piece(k, m, dx, cols):
        return xg.at[m, k, around(y + x + dx + k), :, :, cols]

    def share(ref, k, j, dev):
        push(ref, ref, k, j, dev)

    def share_own(k, m):
        for b in range(2):
            arrived(xg.at[m, k, around(y + x + k), b, :, width(k)], k, PART * m + A2A + b)
        if k > 0:
            share(piece(k, m, 0, mine), k, PART * m + BZ, z_dev)
        for i in range(2):
            share(piece(k, m, 0, mine), k, PART * m + B_OWN + i, x_dev[i])
        if k == 0:
            share_both(k, m)

    def share_both(k, m):
        for i in range(2):
            share(piece(k, m, 0, other), k, PART * m + B_OTHER + i, x_dev[i])

    def share_other(k, m):
        arrived(piece(k, m, 0, other), k, PART * m + BZ)
        share_both(k, m)

    def pass_right(k, m):
        arrived(piece(k, m, -1, mine), k, PART * m + B_OWN)
        share(piece(k, m, -1, mine), k, PART * m + B_FWD, x_dev[0])

    def pass_left(k, m):
        arrived(piece(k, m, 1, other), k, PART * m + B_OTHER + 1)
        share(piece(k, m, 1, other), k, PART * m + B_FWD + 1, x_dev[1])

    def project(k, m):
        if k == 0:
            load(m).wait()
        arrived(piece(k, m, 1, mine), k, PART * m + B_OWN + 1)
        arrived(piece(k, m, -1, other), k, PART * m + B_OTHER)
        arrived(piece(k, m, 2, mine), k, PART * m + B_FWD)
        arrived(piece(k, m, 2, other), k, PART * m + B_FWD + 1)

        def body(n, _):
            cols = pl.ds(pl.multiple_of(n * TILE, TILE), TILE)
            rows = xg[m, k].reshape(NY * 2 * SLOTS, D_LOC)
            if m == 0:
                part = jnp.dot(rows, w_in[:, cols], preferred_element_type=F32)
            else:
                part = lax.dot_general(
                    rows, w_out[cols, :], (((1,), (1,)), ((), ())), preferred_element_type=F32
                )
            ps[k, m, :, :, :, cols] = part.astype(BF16).reshape(NY, 2, SLOTS, TILE)
            return 0

        lax.fori_loop(0, F_LOC // TILE, body, 0)
        far, after, before = (around(y + d) for d in (2, 1, -1))
        j = PART * m
        push(ps.at[k, m, far, 0], r1.at[k, m, 0], k, j + R_FAR, y_dev[0])
        push(ps.at[k, m, far, 1], r1.at[k, m, 1], k, j + R_FAR + 1, y_dev[1])
        push(ps.at[k, m, after, 1], r2.at[k, m, 0, 1], k, j + R_NEAR, y_dev[0])
        push(ps.at[k, m, before, 0], r2.at[k, m, 1, 0], k, j + R_NEAR + 1, y_dev[1])

    def pass_sums(k, m):
        for i in range(2):
            arrived(r1.at[k, m, i], k, PART * m + R_FAR + i)
            to = around(y + 1 - 2 * i)
            total = ps[k, m, to, i].astype(F32) + r1[k, m, i].astype(F32)
            ps[k, m, to, i] = total.astype(BF16)
            push(ps.at[k, m, to, i], r2.at[k, m, i, i], k, PART * m + R_SUM + i, y_dev[i])

    def activate(k):
        for m in range(2):
            for i in range(2):
                arrived(r2.at[k, m, i, 1 - i], k, PART * m + R_NEAR + i)
                arrived(r2.at[k, m, i, i], k, PART * m + R_SUM + i)
        for b in range(2):
            pre, grad = (
                ps[k, m, y, b].astype(F32)
                + r2[k, m, 0, b].astype(F32)
                + r2[k, m, 1, b].astype(F32)
                for m in range(2)
            )
            s = jax.nn.sigmoid(pre)
            hp[0, k, y, b] = (pre * s).astype(BF16)
            hp[1, k, y, b] = (grad * (s * (1.0 + pre * (1.0 - s)))).astype(BF16)
        gather_own(k, 1)

    def gather_own(k, m):
        for i in range(2):
            share(hp.at[m, k, y], k, PART * m + G_OWN + i, y_dev[i])

    def gather_far(k, m):
        for i in range(2):
            near = around(y - 1 + 2 * i)
            arrived(hp.at[m, k, near], k, PART * m + G_OWN + i)
            share(hp.at[m, k, near, i], k, PART * m + G_FWD + i, y_dev[i])

    seen = set()

    def gathered(k, m):
        if (k, m) in seen:
            return
        seen.add((k, m))
        for i in range(2):
            arrived(hp.at[m, k, around(y + 2), i], k, PART * m + G_FWD + i)

    def go_back(k):
        gathered(k, 1)

        def body(n, _):
            cols = pl.ds(pl.multiple_of(n * TILE, TILE), TILE)
            part = lax.dot_general(
                hp[1, k].reshape(NY * 2 * SLOTS, F_LOC),
                w_in[cols, :],
                (((1,), (1,)), ((), ())),
                preferred_element_type=F32,
            )
            bk[k, :, :, :, cols] = part.astype(BF16).reshape(NY, 2, SLOTS, TILE)
            return 0

        lax.fori_loop(0, D_LOC // TILE, body, 0)
        far, after, before = (around(y + x + d) for d in (2, 1, -1))
        push(bk.at[k, far, 0], q1.at[k, 0], k, S_FAR, x_dev[0])
        push(bk.at[k, far, 1], q1.at[k, 1], k, S_FAR + 1, x_dev[1])
        push(bk.at[k, after, 1], q2.at[k, 0, 1], k, S_NEAR, x_dev[0])
        push(bk.at[k, before, 0], q2.at[k, 1, 0], k, S_NEAR + 1, x_dev[1])

    def back_sums(k):
        for i in range(2):
            arrived(q1.at[k, i], k, S_FAR + i)
            to = around(y + x + 1 - 2 * i)
            total = bk[k, to, i].astype(F32) + q1[k, i].astype(F32)
            bk[k, to, i] = total.astype(BF16)
            push(bk.at[k, to, i], q2.at[k, i, i], k, S_SUM + i, x_dev[i])

    def back_across(k):
        for i in range(2):
            arrived(q2.at[k, i, 1 - i], k, S_NEAR + i)
            arrived(q2.at[k, i, i], k, S_SUM + i)
        for b in range(2):
            total = (
                bk[k, y_from, b].astype(F32) + q2[k, 0, b].astype(F32) + q2[k, 1, b].astype(F32)
            )
            bk[k, y_from, b] = total.astype(BF16)
        push(bk.at[k, y_from, :, :, other], q3.at[k], k, S_Z, z_dev)

    def send_home(k):
        arrived(q3.at[k], k, S_Z)
        rb[k] = (bk[k, y_from, :, :, mine].astype(F32) + q3[k].astype(F32)).astype(BF16)
        zs = around(zh + FROM_Z[k])
        for to_core in range(2):
            push_expert(
                rb.at[k, to_core],
                ret.at[2 * k + core],
                k,
                HOME + to_core,
                zs * 2 + to_core,
                y_from,
                HOME + core,
            )

    def weight_in(n):
        for k in range(NZ):
            gathered(k, 1)
        rows = pl.ds(n * TILE, TILE)
        gin[rows, :] = lax.dot_general(
            xg[0, :, :, :, :, rows].reshape(NZ * NY * 2 * SLOTS, TILE),
            hp[1].reshape(NZ * NY * 2 * SLOTS, F_LOC),
            (((0,), (0,)), ((), ())),
            preferred_element_type=F32,
        ).astype(BF16)

    def weight_out(n):
        for k in range(NZ - 1):
            gathered(k, 0)
        rows = pl.ds(n * TILE, TILE)
        acc[rows, :] = lax.dot_general(
            hp[0, : NZ - 1, :, :, :, rows].reshape((NZ - 1) * NY * 2 * SLOTS, TILE),
            xg[1, : NZ - 1].reshape((NZ - 1) * NY * 2 * SLOTS, D_LOC),
            (((0,), (0,)), ((), ())),
            preferred_element_type=F32,
        )

    def weight_out_last(n):
        gathered(NZ - 1, 0)
        rows = pl.ds(n * TILE, TILE)
        part = lax.dot_general(
            hp[0, NZ - 1, :, :, :, rows].reshape(NY * 2 * SLOTS, TILE),
            xg[1, NZ - 1].reshape(NY * 2 * SLOTS, D_LOC),
            (((0,), (0,)), ((), ())),
            preferred_element_type=F32,
        )
        gout[rows, :] = (acc[rows, :] + part).astype(BF16)

    def out_piece(dx, half):
        start = around(y - x - dx) * D_LOC + half * HALF
        return ing.at[:, pl.ds(pl.multiple_of(start, 128), HALF)]

    def out_copy(ref, j, dev):
        return pltpu.make_async_remote_copy(
            src_ref=ref,
            dst_ref=ref,
            send_sem=osend.at[j],
            recv_sem=orecv.at[j],
            device_id=dev,
            device_id_type=MESH,
        )

    def out_push(ref, j, dev):
        copy = out_copy(ref, j, dev)
        copy.start()
        sent.append(copy)

    def out_arrived(ref, j):
        out_copy(ref, j, z_dev).wait_recv()

    def combine():
        for k in range(NZ):
            for b in range(2):
                arrived(ret.at[2 * k + b], k, HOME + b)
        contrib = lax.dot_general(
            comb[0],
            ret[...].reshape(2 * NZ * SLOTS, HALF),
            (((0,), (0,)), ((), ())),
            preferred_element_type=F32,
        )
        start = y_to * D_LOC + c * HALF
        cols = pl.ds(pl.multiple_of(start, 128), HALF)
        ing[:, cols] = (us[:, cols].astype(F32) + contrib).astype(BF16)
        out_push(out_piece(0, c), O_Z, z_dev)
        for i in range(2):
            out_push(out_piece(0, c), O_OWN + i, x_dev[i])

    def out_other():
        out_arrived(out_piece(0, 1 - c), O_Z)
        for i in range(2):
            out_push(out_piece(0, 1 - c), O_OTHER + i, x_dev[i])

    def out_far():
        out_arrived(out_piece(-1, c), O_OWN)
        out_push(out_piece(-1, c), O_FWD, x_dev[0])
        out_arrived(out_piece(1, 1 - c), O_OTHER + 1)
        out_push(out_piece(1, 1 - c), O_FWD + 1, x_dev[1])

    def out_end():
        out_arrived(out_piece(1, c), O_OWN + 1)
        out_arrived(out_piece(-1, 1 - c), O_OTHER)
        out_arrived(out_piece(2, c), O_FWD)
        out_arrived(out_piece(2, 1 - c), O_FWD + 1)

    steps = dict(
        a=share_own,
        b=share_other,
        c=pass_right,
        C=pass_left,
        d=project,
        e=pass_sums,
        f=activate,
        o=lambda k: gather_own(k, 0),
        g=lambda k: gather_far(k, 1),
        q=lambda k: gather_far(k, 0),
        h=go_back,
        i=back_sums,
        j=back_across,
        l=send_home,
        u=weight_in,
        v=weight_out,
        x=weight_out_last,
        s=start_dispatch,
        w=lambda n: (combine, out_other, out_far, out_end)[n](),
    )
    for word in PLAN:
        steps[word[0]](*(int(n) for n in word[1:]))
    for copy in sent:
        copy.wait_send()


def on_device(layer_inputs, out_grad, routes, gates, w_in, w_out):
    tokens = layer_inputs.shape[0]
    vmem = pl.BlockSpec(memory_space=pltpu.VMEM)
    hbm = pl.BlockSpec(memory_space=pl.ANY)
    rows = NY * 2 * SLOTS
    flops = 5 * 2 * NZ * rows * D_LOC * F_LOC
    in_grads, grad_in, grad_out = pl.pallas_call(
        kernel,
        out_shape=(
            pltpu.VMEM(layer_inputs.shape, BF16),
            pltpu.VMEM((D_LOC, F_LOC), BF16),
            pltpu.VMEM((F_LOC, D_LOC), BF16),
        ),
        in_specs=[hbm] * 2 + [vmem] * 2 + [hbm] * 2,
        out_specs=(vmem,) * 3,
        scratch_shapes=[
            pltpu.VMEM((2, NZ, NY, 2, SLOTS, D_LOC), BF16),
            pltpu.VMEM((NZ, 2, NY, 2, SLOTS, F_LOC), BF16),
            pltpu.VMEM((NZ, 2, 2, SLOTS, F_LOC), BF16),
            pltpu.VMEM((NZ, 2, 2, 2, SLOTS, F_LOC), BF16),
            pltpu.VMEM((2, NZ, NY, 2, SLOTS, F_LOC), BF16),
            pltpu.VMEM((NZ, NY, 2, SLOTS, D_LOC), BF16),
            pltpu.VMEM((NZ, 2, SLOTS, D_LOC), BF16),
            pltpu.VMEM((NZ, 2, 2, SLOTS, D_LOC), BF16),
            pltpu.VMEM((NZ, 2, SLOTS, HALF), BF16),
            pltpu.VMEM((NZ, 2, SLOTS, HALF), BF16),
            pltpu.VMEM((2 * NZ, SLOTS, HALF), BF16),
            pltpu.SemaphoreType.DMA((NZ, COPIES)),
            pltpu.SemaphoreType.DMA((NZ, COPIES)),
            pltpu.SemaphoreType.DMA((OUT_COPIES,)),
            pltpu.SemaphoreType.DMA((OUT_COPIES,)),
            pltpu.SemaphoreType.DMA((4,)),
            pltpu.VMEM((D_LOC, F_LOC), BF16),
            pltpu.VMEM((F_LOC, D_LOC), BF16),
            pltpu.VMEM((F_LOC, D_LOC), F32),
            pltpu.VMEM(layer_inputs.shape, BF16),
            pltpu.VMEM(layer_inputs.shape, BF16),
            pltpu.VMEM((2, NZ, 2, SLOTS, D_LOC), BF16),
            pltpu.VMEM((3, 2 * NZ * SLOTS, tokens), BF16),
            pltpu.VMEM((2, tokens, tokens), F32),
        ],
        compiler_params=pltpu.CompilerParams(
            collective_id=0, has_side_effects=True, vmem_limit_bytes=56 * 2**20
        ),
        cost_estimate=pl.CostEstimate(flops=flops, bytes_accessed=2**23, transcendentals=0),
    )(layer_inputs, out_grad, routes.T, gates.T, w_in[0], w_out[0])
    return (in_grads, grad_in[None], grad_out[None])


def solution(mesh):
    assert dict(mesh.shape) == {"section": 2 * NX, "expert": 2 * NZ, "dp": NY}
    return jax.shard_map(
        on_device,
        mesh=mesh,
        in_specs=(
            P(("expert", "dp"), None),
            P(("expert", "dp"), None),
            P(("expert", "dp"), None),
            P(("expert", "dp"), None),
            P("expert", "dp", "section"),
            P("expert", "section", "dp"),
        ),
        out_specs=(
            P(("expert", "dp"), None),
            P("expert", "dp", "section"),
            P("expert", "section", "dp"),
        ),
        check_vma=False,
    )
```

```python
import jax
import jax.numpy as jnp
from jax import lax
from jax.experimental import pallas as pl
from jax.experimental.pallas import tpu as pltpu
from jax.sharding import PartitionSpec as P

MESH = pl.DeviceIdType.MESH
F32 = jnp.float32
BF16 = jnp.bfloat16

ROWS = 64
NX = 4
NY = 4
NZ = 4
SLOTS = 48
D_LOC = 768
HALF = D_LOC // 2
F_LOC = 1024
TILE = 256

FROM_Z = (0, 1, 3, 2)
A2A, BZ, B_OWN, B_OTHER, B_FWD = 0, 2, 3, 5, 7
R_FAR, R_NEAR, R_SUM = 9, 11, 13
G_OWN, G_FWD = 15, 17
PART = 19
S_FAR, S_NEAR, S_SUM, S_Z = 38, 40, 42, 44
HOME = 45
COPIES = 47
O_Z, O_OWN, O_OTHER, O_FWD = 0, 1, 3, 5
OUT_COPIES = 7
PLAN = (
    "s01", "s00", "s10", "s31", "a01", "s20", "s11", "s30", "a00", "C01", "c01", "a20", "C00", "c00",
    "s21", "d01", "a31", "b20", "d00", "a21", "c20", "b31", "e01", "C20", "b21", "a30", "C31", "e00",
    "c31", "d20", "a10", "c21", "C21", "b30", "a11", "d31", "b11", "d21", "c10", "C30", "b10", "e31",
    "C10", "e20", "C11", "c11", "e21", "d10", "d11", "e10", "c30", "d30", "f2", "e11", "e30", "g2",
    "f1", "f3", "g1", "h2", "f0", "g3", "i2", "h1", "g0", "i1", "o0", "o2", "j2", "h3",
    "j1", "h0", "u2", "l1", "i3", "i0", "o1", "u1", "j3", "l2", "q2", "j0", "u0", "l3",
    "l0", "q1", "o3", "w0", "q0", "w1", "q3", "w2", "v2", "v3", "v0", "x0", "v1", "x1",
    "x2", "x3", "w3",
)


def kernel(
    x_ref,
    up_ref,
    routes_ref,
    gates_ref,
    w_in_ref,
    w_out_ref,
    ing,
    gin,
    gout,
    xg,
    ps,
    r1,
    r2,
    hp,
    bk,
    q1,
    q2,
    q3,
    rb,
    ret,
    ssem,
    rsem,
    osend,
    orecv,
    lsem,
    w_in,
    w_out,
    acc,
    xs,
    us,
    send,
    comb,
    gate,
):
    section = lax.axis_index("section")
    expert = lax.axis_index("expert")
    y = lax.axis_index("dp")
    x, c = lax.rem(section, NX), section // NX
    zh, core = expert // 2, lax.rem(expert, 2)

    def around(value, n=4):
        return lax.rem(value + 2 * n, n)

    x_dev = (
        {"section": c * NX + around(x + 1)},
        {"section": c * NX + around(x - 1)},
    )
    z_dev = {"section": (1 - c) * NX + x}
    y_dev = ({"dp": around(y + 1)}, {"dp": around(y - 1)})
    y_to = around(y - x)
    y_from = around(y + x)
    mine = pl.ds(pl.multiple_of(c * HALF, 128), HALF)
    other = pl.ds(pl.multiple_of((1 - c) * HALF, 128), HALF)

    def load(n):
        src, dst = (
            (w_in_ref, w_in),
            (w_out_ref, w_out),
            (x_ref, xs),
            (up_ref, us),
        )[n]
        return pltpu.make_async_copy(src, dst, lsem.at[n])

    for n in (2, 3, 0, 1):
        load(n).start()
    barrier = pltpu.get_barrier_semaphore()
    for dev in x_dev + y_dev + (z_dev,):
        pl.semaphore_signal(barrier, inc=1, device_id=dev, device_id_type=MESH)
    for k in range(NZ):
        ahead, behind = around(zh + FROM_Z[k]), around(zh - FROM_Z[k])
        pairs = [(behind, around(y - x - k)), (ahead, around(y + x + k))]
        if k > 0:
            pairs += [(ahead, y_from), (behind, y_to)]
        for to_core in range(2):
            for zz, yy in pairs:

                def greet(e=zz * 2 + to_core, yy=yy):
                    pl.semaphore_signal(
                        barrier,
                        inc=1,
                        device_id={"expert": e, "dp": yy},
                        device_id_type=MESH,
                    )

                if k > 0:
                    greet()
                else:
                    pl.when(jnp.logical_or(x != 0, core != to_core))(greet)

    tokens, count = us.shape[0], 2 * NZ * SLOTS
    place = lax.broadcasted_iota(jnp.int32, (count, tokens), 0)
    expert_of, slot = jnp.zeros_like(place), place
    for k in range(NZ):
        for b in range(2):
            start = (2 * k + b) * SLOTS
            here = place >= start
            expert_of = jnp.where(here, around(zh - FROM_Z[k]) * 2 + b, expert_of)
            slot = jnp.where(here, place - start, slot)
    token = lax.broadcasted_iota(jnp.int32, (count, tokens), 1)
    slot = slot - jnp.where(token >= ROWS, SLOTS // 2, 0)
    is_first = routes_ref[0:1, :] == expert_of
    is_second = routes_ref[1:2, :] == expert_of
    named = jnp.logical_or(is_first, is_second)
    row = lax.broadcasted_iota(jnp.int32, (tokens, tokens), 0)
    col = lax.broadcasted_iota(jnp.int32, (tokens, tokens), 1)
    earlier = jnp.logical_and(row < col, row >= jnp.where(col >= ROWS, ROWS, 0))

    def ones(mask):
        return jnp.where(mask, 1.0, 0.0).astype(BF16)

    before = jnp.dot(ones(named), ones(earlier), preferred_element_type=F32)
    taken = jnp.logical_and(named, before == slot.astype(F32))
    comb[0] = ones(taken)
    comb[1] = ones(jnp.logical_and(taken, is_first))
    comb[2] = ones(jnp.logical_and(taken, is_second))
    for i in range(2):
        gate[i] = jnp.broadcast_to(gates_ref[i : i + 1, :], (tokens, tokens)).T
    load(2).wait()
    load(3).wait()

    def pick(k, m):
        rows = pl.ds(2 * k * SLOTS, 2 * SLOTS)
        first = around(y - x - k) * D_LOC
        for half in (0, 1) if k == 0 else (c,):
            cols = pl.ds(pl.multiple_of(first + half * HALF, 128), HALF)
            if m == 0:
                part = jnp.dot(comb[0, rows], xs[:, cols], preferred_element_type=F32)
            else:
                part = 0.0
                wide = us[:, cols].astype(F32)
                for i in range(2):
                    weight = jnp.concatenate([gate[i]] * (HALF // tokens), axis=1)
                    part = part + jnp.dot(
                        comb[1 + i, rows],
                        (weight * wide).astype(BF16),
                        preferred_element_type=F32,
                    )
            place_in = pl.ds(half * HALF, HALF) if k == 0 else mine
            send[m, k, :, :, place_in] = part.astype(BF16).reshape(2, SLOTS, HALF)

    pick(0, 0)
    pl.semaphore_wait(barrier, jnp.where(x == 0, 31, 33))

    sent = []

    def remote(src, dst, k, j, dev, rj=None):
        return pltpu.make_async_remote_copy(
            src_ref=src,
            dst_ref=dst,
            send_sem=ssem.at[k, j],
            recv_sem=rsem.at[k, j if rj is None else rj],
            device_id=dev,
            device_id_type=MESH,
        )

    def push(src, dst, k, j, dev, rj=None):
        copy = remote(src, dst, k, j, dev, rj)
        copy.start()
        sent.append(copy)

    def arrived(dst, k, j):
        remote(dst, dst, k, j, z_dev).wait_recv()

    def push_expert(src, dst, k, j, e, yy, rj):
        if k != 0:
            push(src, dst, k, j, {"expert": e, "dp": yy}, rj)
            return
        own = jnp.logical_and(x == 0, expert == e)
        copy = remote(src, dst, k, j, {"expert": e, "dp": yy}, rj)
        local = pltpu.make_async_copy(src, dst, rsem.at[k, rj])

        @pl.when(own)
        def _():
            local.start()

        @pl.when(jnp.logical_not(own))
        def _():
            copy.start()

        class Guarded:
            def wait_send(self):
                @pl.when(jnp.logical_not(own))
                def _():
                    copy.wait_send()

        sent.append(Guarded())

    def width(k):
        return pl.ds(0, D_LOC) if k == 0 else mine

    def start_dispatch(k, m):
        if (k, m) != (0, 0):
            pick(k, m)
        zd = around(zh - FROM_Z[k])
        for to_core in range(2):
            e = zd * 2 + to_core
            push_expert(
                send.at[m, k, to_core, :, width(k)],
                xg.at[m, k, y, core, :, width(k)],
                k,
                PART * m + A2A + to_core,
                e,
                around(y - x - k),
                PART * m + A2A + core,
            )

    def piece(k, m, dx, cols):
        return xg.at[m, k, around(y + x + dx + k), :, :, cols]

    def share(ref, k, j, dev):
        push(ref, ref, k, j, dev)

    def share_own(k, m):
        for b in range(2):
            arrived(xg.at[m, k, around(y + x + k), b, :, width(k)], k, PART * m + A2A + b)
        if k > 0:
            share(piece(k, m, 0, mine), k, PART * m + BZ, z_dev)
        for i in range(2):
            share(piece(k, m, 0, mine), k, PART * m + B_OWN + i, x_dev[i])
        if k == 0:
            share_both(k, m)

    def share_both(k, m):
        for i in range(2):
            share(piece(k, m, 0, other), k, PART * m + B_OTHER + i, x_dev[i])

    def share_other(k, m):
        arrived(piece(k, m, 0, other), k, PART * m + BZ)
        share_both(k, m)

    def pass_right(k, m):
        arrived(piece(k, m, -1, mine), k, PART * m + B_OWN)
        share(piece(k, m, -1, mine), k, PART * m + B_FWD, x_dev[0])

    def pass_left(k, m):
        arrived(piece(k, m, 1, other), k, PART * m + B_OTHER + 1)
        share(piece(k, m, 1, other), k, PART * m + B_FWD + 1, x_dev[1])

    def project(k, m):
        if k == 0:
            load(m).wait()
        arrived(piece(k, m, 1, mine), k, PART * m + B_OWN + 1)
        arrived(piece(k, m, -1, other), k, PART * m + B_OTHER)
        arrived(piece(k, m, 2, mine), k, PART * m + B_FWD)
        arrived(piece(k, m, 2, other), k, PART * m + B_FWD + 1)

        def body(n, _):
            cols = pl.ds(pl.multiple_of(n * TILE, TILE), TILE)
            rows = xg[m, k].reshape(NY * 2 * SLOTS, D_LOC)
            if m == 0:
                part = jnp.dot(rows, w_in[:, cols], preferred_element_type=F32)
            else:
                part = lax.dot_general(
                    rows, w_out[cols, :], (((1,), (1,)), ((), ())), preferred_element_type=F32
                )
            ps[k, m, :, :, :, cols] = part.astype(BF16).reshape(NY, 2, SLOTS, TILE)
            return 0

        lax.fori_loop(0, F_LOC // TILE, body, 0, unroll=True)
        far, after, before = (around(y + d) for d in (2, 1, -1))
        j = PART * m
        push(ps.at[k, m, far, 0], r1.at[k, m, 0], k, j + R_FAR, y_dev[0])
        push(ps.at[k, m, far, 1], r1.at[k, m, 1], k, j + R_FAR + 1, y_dev[1])
        push(ps.at[k, m, after, 1], r2.at[k, m, 0, 1], k, j + R_NEAR, y_dev[0])
        push(ps.at[k, m, before, 0], r2.at[k, m, 1, 0], k, j + R_NEAR + 1, y_dev[1])

    def pass_sums(k, m):
        for i in range(2):
            arrived(r1.at[k, m, i], k, PART * m + R_FAR + i)
            to = around(y + 1 - 2 * i)
            total = ps[k, m, to, i].astype(F32) + r1[k, m, i].astype(F32)
            ps[k, m, to, i] = total.astype(BF16)
            push(ps.at[k, m, to, i], r2.at[k, m, i, i], k, PART * m + R_SUM + i, y_dev[i])

    def activate(k):
        for m in range(2):
            for i in range(2):
                arrived(r2.at[k, m, i, 1 - i], k, PART * m + R_NEAR + i)
                arrived(r2.at[k, m, i, i], k, PART * m + R_SUM + i)
        for b in range(2):
            pre, grad = (
                ps[k, m, y, b].astype(F32)
                + r2[k, m, 0, b].astype(F32)
                + r2[k, m, 1, b].astype(F32)
                for m in range(2)
            )
            s = jax.nn.sigmoid(pre)
            hp[0, k, y, b] = (pre * s).astype(BF16)
            hp[1, k, y, b] = (grad * (s * (1.0 + pre * (1.0 - s)))).astype(BF16)
        gather_own(k, 1)

    def gather_own(k, m):
        for i in range(2):
            share(hp.at[m, k, y], k, PART * m + G_OWN + i, y_dev[i])

    def gather_far(k, m):
        for i in range(2):
            near = around(y - 1 + 2 * i)
            arrived(hp.at[m, k, near], k, PART * m + G_OWN + i)
            share(hp.at[m, k, near, i], k, PART * m + G_FWD + i, y_dev[i])

    seen = set()

    def gathered(k, m):
        if (k, m) in seen:
            return
        seen.add((k, m))
        for i in range(2):
            arrived(hp.at[m, k, around(y + 2), i], k, PART * m + G_FWD + i)

    def go_back(k):
        gathered(k, 1)

        def body(n, _):
            cols = pl.ds(pl.multiple_of(n * TILE, TILE), TILE)
            part = lax.dot_general(
                hp[1, k].reshape(NY * 2 * SLOTS, F_LOC),
                w_in[cols, :],
                (((1,), (1,)), ((), ())),
                preferred_element_type=F32,
            )
            bk[k, :, :, :, cols] = part.astype(BF16).reshape(NY, 2, SLOTS, TILE)
            return 0

        lax.fori_loop(0, D_LOC // TILE, body, 0, unroll=True)
        far, after, before = (around(y + x + d) for d in (2, 1, -1))
        push(bk.at[k, far, 0], q1.at[k, 0], k, S_FAR, x_dev[0])
        push(bk.at[k, far, 1], q1.at[k, 1], k, S_FAR + 1, x_dev[1])
        push(bk.at[k, after, 1], q2.at[k, 0, 1], k, S_NEAR, x_dev[0])
        push(bk.at[k, before, 0], q2.at[k, 1, 0], k, S_NEAR + 1, x_dev[1])

    def back_sums(k):
        for i in range(2):
            arrived(q1.at[k, i], k, S_FAR + i)
            to = around(y + x + 1 - 2 * i)
            total = bk[k, to, i].astype(F32) + q1[k, i].astype(F32)
            bk[k, to, i] = total.astype(BF16)
            push(bk.at[k, to, i], q2.at[k, i, i], k, S_SUM + i, x_dev[i])

    def back_across(k):
        for i in range(2):
            arrived(q2.at[k, i, 1 - i], k, S_NEAR + i)
            arrived(q2.at[k, i, i], k, S_SUM + i)
        for b in range(2):
            total = (
                bk[k, y_from, b].astype(F32) + q2[k, 0, b].astype(F32) + q2[k, 1, b].astype(F32)
            )
            bk[k, y_from, b] = total.astype(BF16)
        push(bk.at[k, y_from, :, :, other], q3.at[k], k, S_Z, z_dev)

    def send_home(k):
        arrived(q3.at[k], k, S_Z)
        rb[k] = (bk[k, y_from, :, :, mine].astype(F32) + q3[k].astype(F32)).astype(BF16)
        zs = around(zh + FROM_Z[k])
        for to_core in range(2):
            push_expert(
                rb.at[k, to_core],
                ret.at[2 * k + core],
                k,
                HOME + to_core,
                zs * 2 + to_core,
                y_from,
                HOME + core,
            )

    def weight_in(n):
        for k in range(NZ):
            gathered(k, 1)
        rows = pl.ds(n * TILE, TILE)
        gin[rows, :] = lax.dot_general(
            xg[0, :, :, :, :, rows].reshape(NZ * NY * 2 * SLOTS, TILE),
            hp[1].reshape(NZ * NY * 2 * SLOTS, F_LOC),
            (((0,), (0,)), ((), ())),
            preferred_element_type=F32,
        ).astype(BF16)

    def weight_out(n):
        for k in range(NZ - 1):
            gathered(k, 0)
        rows = pl.ds(n * TILE, TILE)
        acc[rows, :] = lax.dot_general(
            hp[0, : NZ - 1, :, :, :, rows].reshape((NZ - 1) * NY * 2 * SLOTS, TILE),
            xg[1, : NZ - 1].reshape((NZ - 1) * NY * 2 * SLOTS, D_LOC),
            (((0,), (0,)), ((), ())),
            preferred_element_type=F32,
        )

    def weight_out_last(n):
        gathered(NZ - 1, 0)
        rows = pl.ds(n * TILE, TILE)
        part = lax.dot_general(
            hp[0, NZ - 1, :, :, :, rows].reshape(NY * 2 * SLOTS, TILE),
            xg[1, NZ - 1].reshape(NY * 2 * SLOTS, D_LOC),
            (((0,), (0,)), ((), ())),
            preferred_element_type=F32,
        )
        gout[rows, :] = (acc[rows, :] + part).astype(BF16)

    def out_piece(dx, half):
        start = around(y - x - dx) * D_LOC + half * HALF
        return ing.at[:, pl.ds(pl.multiple_of(start, 128), HALF)]

    def out_copy(ref, j, dev):
        return pltpu.make_async_remote_copy(
            src_ref=ref,
            dst_ref=ref,
            send_sem=osend.at[j],
            recv_sem=orecv.at[j],
            device_id=dev,
            device_id_type=MESH,
        )

    def out_push(ref, j, dev):
        copy = out_copy(ref, j, dev)
        copy.start()
        sent.append(copy)

    def out_arrived(ref, j):
        out_copy(ref, j, z_dev).wait_recv()

    def combine():
        for k in range(NZ):
            for b in range(2):
                arrived(ret.at[2 * k + b], k, HOME + b)
        contrib = lax.dot_general(
            comb[0],
            ret[...].reshape(2 * NZ * SLOTS, HALF),
            (((0,), (0,)), ((), ())),
            preferred_element_type=F32,
        )
        start = y_to * D_LOC + c * HALF
        cols = pl.ds(pl.multiple_of(start, 128), HALF)
        ing[:, cols] = (us[:, cols].astype(F32) + contrib).astype(BF16)
        out_push(out_piece(0, c), O_Z, z_dev)
        for i in range(2):
            out_push(out_piece(0, c), O_OWN + i, x_dev[i])

    def out_other():
        out_arrived(out_piece(0, 1 - c), O_Z)
        for i in range(2):
            out_push(out_piece(0, 1 - c), O_OTHER + i, x_dev[i])

    def out_far():
        out_arrived(out_piece(-1, c), O_OWN)
        out_push(out_piece(-1, c), O_FWD, x_dev[0])
        out_arrived(out_piece(1, 1 - c), O_OTHER + 1)
        out_push(out_piece(1, 1 - c), O_FWD + 1, x_dev[1])

    def out_end():
        out_arrived(out_piece(1, c), O_OWN + 1)
        out_arrived(out_piece(-1, 1 - c), O_OTHER)
        out_arrived(out_piece(2, c), O_FWD)
        out_arrived(out_piece(2, 1 - c), O_FWD + 1)

    steps = dict(
        a=share_own,
        b=share_other,
        c=pass_right,
        C=pass_left,
        d=project,
        e=pass_sums,
        f=activate,
        o=lambda k: gather_own(k, 0),
        g=lambda k: gather_far(k, 1),
        q=lambda k: gather_far(k, 0),
        h=go_back,
        i=back_sums,
        j=back_across,
        l=send_home,
        u=weight_in,
        v=weight_out,
        x=weight_out_last,
        s=start_dispatch,
        w=lambda n: (combine, out_other, out_far, out_end)[n](),
    )
    for word in PLAN:
        steps[word[0]](*(int(n) for n in word[1:]))
    for copy in sent:
        copy.wait_send()


def store_kernel(*refs):
    *pairs, sem = refs
    copies = []
    for i in range(3):
        src, dst = pairs[i], pairs[3 + i]
        rows = src.shape[0] // 4
        for n in range(4):
            part = pl.ds(n * rows, rows)
            copies.append(pltpu.make_async_copy(src.at[part], dst.at[part], sem.at[4 * i + n]))
    for copy in copies:
        copy.start()
    for copy in copies:
        copy.wait()


def store_results(*arrays):
    hbm = pl.BlockSpec(memory_space=pl.ANY)
    size = sum(a.size * a.dtype.itemsize for a in arrays)
    return pl.pallas_call(
        store_kernel,
        out_shape=tuple(jax.ShapeDtypeStruct(a.shape, a.dtype) for a in arrays),
        in_specs=[hbm] * 3,
        out_specs=(hbm,) * 3,
        scratch_shapes=[pltpu.SemaphoreType.DMA((12,))],
        compiler_params=pltpu.CompilerParams(vmem_limit_bytes=2**20),
        cost_estimate=pl.CostEstimate(flops=0, bytes_accessed=size, transcendentals=0),
    )(*(pltpu.with_memory_space_constraint(a, pltpu.VMEM) for a in arrays))


def on_device(layer_inputs, out_grad, routes, gates, w_in, w_out):
    tokens = layer_inputs.shape[0]
    vmem = pl.BlockSpec(memory_space=pltpu.VMEM)
    hbm = pl.BlockSpec(memory_space=pl.ANY)
    rows = NY * 2 * SLOTS
    flops = 5 * 2 * NZ * rows * D_LOC * F_LOC
    in_grads, grad_in, grad_out = pl.pallas_call(
        kernel,
        out_shape=(
            pltpu.VMEM(layer_inputs.shape, BF16),
            pltpu.VMEM((D_LOC, F_LOC), BF16),
            pltpu.VMEM((F_LOC, D_LOC), BF16),
        ),
        in_specs=[hbm] * 2 + [vmem] * 2 + [hbm] * 2,
        out_specs=(vmem,) * 3,
        scratch_shapes=[
            pltpu.VMEM((2, NZ, NY, 2, SLOTS, D_LOC), BF16),
            pltpu.VMEM((NZ, 2, NY, 2, SLOTS, F_LOC), BF16),
            pltpu.VMEM((NZ, 2, 2, SLOTS, F_LOC), BF16),
            pltpu.VMEM((NZ, 2, 2, 2, SLOTS, F_LOC), BF16),
            pltpu.VMEM((2, NZ, NY, 2, SLOTS, F_LOC), BF16),
            pltpu.VMEM((NZ, NY, 2, SLOTS, D_LOC), BF16),
            pltpu.VMEM((NZ, 2, SLOTS, D_LOC), BF16),
            pltpu.VMEM((NZ, 2, 2, SLOTS, D_LOC), BF16),
            pltpu.VMEM((NZ, 2, SLOTS, HALF), BF16),
            pltpu.VMEM((NZ, 2, SLOTS, HALF), BF16),
            pltpu.VMEM((2 * NZ, SLOTS, HALF), BF16),
            pltpu.SemaphoreType.DMA((NZ, COPIES)),
            pltpu.SemaphoreType.DMA((NZ, COPIES)),
            pltpu.SemaphoreType.DMA((OUT_COPIES,)),
            pltpu.SemaphoreType.DMA((OUT_COPIES,)),
            pltpu.SemaphoreType.DMA((4,)),
            pltpu.VMEM((D_LOC, F_LOC), BF16),
            pltpu.VMEM((F_LOC, D_LOC), BF16),
            pltpu.VMEM((F_LOC, D_LOC), F32),
            pltpu.VMEM(layer_inputs.shape, BF16),
            pltpu.VMEM(layer_inputs.shape, BF16),
            pltpu.VMEM((2, NZ, 2, SLOTS, D_LOC), BF16),
            pltpu.VMEM((3, 2 * NZ * SLOTS, tokens), BF16),
            pltpu.VMEM((2, tokens, tokens), F32),
        ],
        compiler_params=pltpu.CompilerParams(
            collective_id=0, has_side_effects=True, vmem_limit_bytes=50 * 2**20
        ),
        cost_estimate=pl.CostEstimate(flops=flops, bytes_accessed=2**23, transcendentals=0),
    )(layer_inputs, out_grad, routes.T, gates.T, w_in[0], w_out[0])
    in_grads, grad_in, grad_out = store_results(in_grads, grad_in, grad_out)
    return (in_grads, grad_in[None], grad_out[None])


def solution(mesh):
    assert dict(mesh.shape) == {"section": 2 * NX, "expert": 2 * NZ, "dp": NY}
    return jax.shard_map(
        on_device,
        mesh=mesh,
        in_specs=(
            P(("expert", "dp"), None),
            P(("expert", "dp"), None),
            P(("expert", "dp"), None),
            P(("expert", "dp"), None),
            P("expert", "dp", "section"),
            P("expert", "section", "dp"),
        ),
        out_specs=(
            P(("expert", "dp"), None),
            P("expert", "dp", "section"),
            P("expert", "section", "dp"),
        ),
        check_vma=False,
    )
```

```python
import jax
import jax.numpy as jnp
from jax import lax
from jax.experimental import pallas as pl
from jax.experimental.pallas import tpu as pltpu
from jax.sharding import PartitionSpec as P

MESH = pl.DeviceIdType.MESH
F32 = jnp.float32
BF16 = jnp.bfloat16

ROWS = 64
NX = 4
NY = 4
NZ = 4
SLOTS = 48
D_LOC = 768
HALF = D_LOC // 2
F_LOC = 1024
TILE = 256

FROM_Z = (0, 1, 3, 2)
A2A, BZ, B_OWN, B_OTHER, B_FWD = 0, 2, 3, 5, 7
R_FAR, R_NEAR, R_SUM = 9, 11, 13
G_OWN, G_FWD = 15, 17
PART = 19
S_FAR, S_NEAR, S_SUM = 38, 40, 42
S_PART = 6
S_Z = 50
HOME = 51
COPIES = 53
O_Z, O_OWN, O_OTHER, O_FWD = 0, 2, 4, 8
OUT_COPIES = 12
PLAN = (
    "s00", "s20", "s01", "s11", "s30", "a001", "a000", "a011", "s21", "c001", "C001", "a20",
    "s31", "c000", "s10", "C000", "C011", "c011", "d001", "a010", "b20", "a21", "d000", "d011",
    "C010", "c010", "c20", "C20", "e001", "e000", "d010", "b21", "c21", "a11", "d20", "C21",
    "b11", "a10", "e011", "a31", "e010", "d21", "C11", "b10", "e200", "e201", "c11", "a30",
    "e211", "e210", "b30", "b31", "d11", "C10", "c30", "f2", "c31", "c10", "C31", "e111",
    "d10", "d31", "e100", "g2", "e110", "e101", "C30", "d30", "e311", "e300", "e301", "h2",
    "e310", "f1", "f3", "i21", "g1", "i20", "f0", "g3", "h1", "o1", "j2", "i10",
    "h3", "g0", "i30", "o0", "j1", "o2", "i11", "h0", "l1", "u1", "j3", "i00",
    "l2", "i01", "i31", "q0", "j0", "u0", "l3", "l0", "o3", "w0", "q2", "q1",
    "w10", "q3", "w11", "u2", "w30", "w2", "w31", "v2", "v1", "v0", "v3", "x0",
    "x3", "x1", "x2", "w4",
)


def kernel(
    x_ref,
    up_ref,
    routes_ref,
    gates_ref,
    w_in_ref,
    w_out_ref,
    ing,
    gin,
    gout,
    xg,
    ps,
    r1,
    r2,
    hp,
    bk,
    q1,
    q2,
    q3,
    rb,
    ret,
    ssem,
    rsem,
    osend,
    orecv,
    lsem,
    w_in,
    w_out,
    acc,
    xs,
    us,
    send,
    comb,
    gate,
):
    section = lax.axis_index("section")
    expert = lax.axis_index("expert")
    y = lax.axis_index("dp")
    x, c = lax.rem(section, NX), section // NX
    zh, core = expert // 2, lax.rem(expert, 2)

    def around(value, n=4):
        return lax.rem(value + 2 * n, n)

    x_dev = (
        {"section": c * NX + around(x + 1)},
        {"section": c * NX + around(x - 1)},
    )
    z_dev = {"section": (1 - c) * NX + x}
    y_dev = ({"dp": around(y + 1)}, {"dp": around(y - 1)})
    y_to = around(y - x)
    y_from = around(y + x)
    mine = pl.ds(pl.multiple_of(c * HALF, 128), HALF)
    other = pl.ds(pl.multiple_of((1 - c) * HALF, 128), HALF)

    def shift(k):
        return x + k + 2

    def load(n):
        src, dst = (
            (w_in_ref, w_in),
            (w_out_ref, w_out),
            (x_ref, xs),
            (up_ref, us),
        )[n]
        return pltpu.make_async_copy(src, dst, lsem.at[n])

    for n in (2, 3, 0, 1):
        load(n).start()
    barrier = pltpu.get_barrier_semaphore()
    for dev in x_dev + y_dev + (z_dev,):
        pl.semaphore_signal(barrier, inc=1, device_id=dev, device_id_type=MESH)
    for k in range(NZ):
        ahead, behind = around(zh + FROM_Z[k]), around(zh - FROM_Z[k])
        pairs = [
            (behind, around(y - shift(k)), k > 0 or around(shift(k)) != 0),
            (ahead, around(y + shift(k)), k > 0 or around(shift(k)) != 0),
            (ahead, y_from, k > 0 or x != 0),
            (behind, y_to, k > 0 or x != 0),
        ]
        for to_core in range(2):
            for zz, yy, away in pairs:

                def greet(e=zz * 2 + to_core, yy=yy):
                    pl.semaphore_signal(
                        barrier,
                        inc=1,
                        device_id={"expert": e, "dp": yy},
                        device_id_type=MESH,
                    )

                if k > 0:
                    greet()
                else:
                    pl.when(jnp.logical_or(away, core != to_core))(greet)

    tokens, count = us.shape[0], 2 * NZ * SLOTS
    place = lax.broadcasted_iota(jnp.int32, (count, tokens), 0)
    expert_of, slot = jnp.zeros_like(place), place
    for k in range(NZ):
        for b in range(2):
            start = (2 * k + b) * SLOTS
            here = place >= start
            expert_of = jnp.where(here, around(zh - FROM_Z[k]) * 2 + b, expert_of)
            slot = jnp.where(here, place - start, slot)
    token = lax.broadcasted_iota(jnp.int32, (count, tokens), 1)
    slot = slot - jnp.where(token >= ROWS, SLOTS // 2, 0)
    is_first = routes_ref[0:1, :] == expert_of
    is_second = routes_ref[1:2, :] == expert_of
    named = jnp.logical_or(is_first, is_second)
    row = lax.broadcasted_iota(jnp.int32, (tokens, tokens), 0)
    col = lax.broadcasted_iota(jnp.int32, (tokens, tokens), 1)
    earlier = jnp.logical_and(row < col, row >= jnp.where(col >= ROWS, ROWS, 0))

    def ones(mask):
        return jnp.where(mask, 1.0, 0.0).astype(BF16)

    before = jnp.dot(ones(named), ones(earlier), preferred_element_type=F32)
    taken = jnp.logical_and(named, before == slot.astype(F32))
    comb[0] = ones(taken)
    load(2).wait()

    prepared = []

    def prepare_grads():
        for i, mask in enumerate((is_first, is_second)):
            comb[1 + i] = ones(jnp.logical_and(taken, mask))
            gate[i] = jnp.broadcast_to(gates_ref[i : i + 1, :], (tokens, tokens)).T
        load(3).wait()

    def pick(k, m):
        rows = pl.ds(2 * k * SLOTS, 2 * SLOTS)
        first = around(y - shift(k)) * D_LOC
        for half in (0, 1) if k == 0 else (c,):
            cols = pl.ds(pl.multiple_of(first + half * HALF, 128), HALF)
            if m == 0:
                part = jnp.dot(comb[0, rows], xs[:, cols], preferred_element_type=F32)
            else:
                part = 0.0
                wide = us[:, cols].astype(F32)
                for i in range(2):
                    weight = jnp.concatenate([gate[i]] * (HALF // tokens), axis=1)
                    part = part + jnp.dot(
                        comb[1 + i, rows],
                        (weight * wide).astype(BF16),
                        preferred_element_type=F32,
                    )
            place_in = pl.ds(half * HALF, HALF) if k == 0 else mine
            send[m, k, :, :, place_in] = part.astype(BF16).reshape(2, SLOTS, HALF)

    pick(0, 0)
    pl.semaphore_wait(barrier, jnp.where(lax.rem(x, 2) == 0, 35, 37))

    sent = []

    def remote(src, dst, k, j, dev, rj=None):
        return pltpu.make_async_remote_copy(
            src_ref=src,
            dst_ref=dst,
            send_sem=ssem.at[k, j],
            recv_sem=rsem.at[k, j if rj is None else rj],
            device_id=dev,
            device_id_type=MESH,
        )

    def push(src, dst, k, j, dev, rj=None):
        copy = remote(src, dst, k, j, dev, rj)
        copy.start()
        sent.append(copy)

    def arrived(dst, k, j):
        remote(dst, dst, k, j, z_dev).wait_recv()

    def push_expert(src, dst, k, j, e, yy, rj, level):
        if k != 0:
            push(src, dst, k, j, {"expert": e, "dp": yy}, rj)
            return
        own = jnp.logical_and(level, expert == e)
        copy = remote(src, dst, k, j, {"expert": e, "dp": yy}, rj)
        local = pltpu.make_async_copy(src, dst, rsem.at[k, rj])

        @pl.when(own)
        def _():
            local.start()

        @pl.when(jnp.logical_not(own))
        def _():
            copy.start()

        class Guarded:
            def wait_send(self):
                @pl.when(jnp.logical_not(own))
                def _():
                    copy.wait_send()

        sent.append(Guarded())

    def width(k):
        return pl.ds(0, D_LOC) if k == 0 else mine

    def start_dispatch(k, m):
        if m == 1 and not prepared:
            prepared.append(True)
            prepare_grads()
        if (k, m) != (0, 0):
            pick(k, m)
        zd = around(zh - FROM_Z[k])
        for to_core in range(2):
            e = zd * 2 + to_core
            push_expert(
                send.at[m, k, to_core, :, width(k)],
                xg.at[m, k, y, core, :, width(k)],
                k,
                PART * m + A2A + to_core,
                e,
                around(y - shift(k)),
                PART * m + A2A + core,
                around(shift(k)) == 0,
            )

    def piece(k, m, dx, cols, b):
        return xg.at[m, k, around(y + dx + shift(k)), slice(None) if b is None else b, :, cols]

    def sems(k, b):
        return NZ if b == 1 else k

    def share(ref, k, j, dev):
        push(ref, ref, k, j, dev)

    def share_own(k, m, b=None):
        for i in (0, 1) if b is None else (b,):
            rows = xg.at[m, k, around(y + shift(k)), i, :, width(k)]
            arrived(rows, k, PART * m + A2A + i)
        if k > 0:
            share(piece(k, m, 0, mine, b), k, PART * m + BZ, z_dev)
        for i in range(2):
            share(piece(k, m, 0, mine, b), sems(k, b), PART * m + B_OWN + i, x_dev[i])
        if k == 0:
            share_both(k, m, b)

    def share_both(k, m, b=None):
        for i in range(2):
            share(piece(k, m, 0, other, b), sems(k, b), PART * m + B_OTHER + i, x_dev[i])

    def share_other(k, m):
        arrived(piece(k, m, 0, other, None), k, PART * m + BZ)
        share_both(k, m)

    def pass_right(k, m, b=None):
        arrived(piece(k, m, -1, mine, b), sems(k, b), PART * m + B_OWN)
        share(piece(k, m, -1, mine, b), sems(k, b), PART * m + B_FWD, x_dev[0])

    def pass_left(k, m, b=None):
        arrived(piece(k, m, 1, other, b), sems(k, b), PART * m + B_OTHER + 1)
        share(piece(k, m, 1, other, b), sems(k, b), PART * m + B_FWD + 1, x_dev[1])

    loaded = set()

    def project(k, m, b=None):
        if m not in loaded:
            loaded.add(m)
            load(m).wait()
        arrived(piece(k, m, 1, mine, b), sems(k, b), PART * m + B_OWN + 1)
        arrived(piece(k, m, -1, other, b), sems(k, b), PART * m + B_OTHER)
        arrived(piece(k, m, 2, mine, b), sems(k, b), PART * m + B_FWD)
        arrived(piece(k, m, 2, other, b), sems(k, b), PART * m + B_FWD + 1)
        which = slice(None) if b is None else slice(b, b + 1)
        count = 2 if b is None else 1

        def body(n, _):
            cols = pl.ds(pl.multiple_of(n * TILE, TILE), TILE)
            rows = xg[m, k, :, which].reshape(NY * count * SLOTS, D_LOC)
            if m == 0:
                part = jnp.dot(rows, w_in[:, cols], preferred_element_type=F32)
            else:
                part = lax.dot_general(
                    rows, w_out[cols, :], (((1,), (1,)), ((), ())), preferred_element_type=F32
                )
            ps[k, m, :, which, :, cols] = part.astype(BF16).reshape(NY, count, SLOTS, TILE)
            return 0

        lax.fori_loop(0, F_LOC // TILE, body, 0, unroll=True)
        far, after, before = (around(y + d) for d in (2, 1, -1))
        j = PART * m
        if b != 1:
            push(ps.at[k, m, far, 0], r1.at[k, m, 0], k, j + R_FAR, y_dev[0])
        if b != 0:
            push(ps.at[k, m, far, 1], r1.at[k, m, 1], k, j + R_FAR + 1, y_dev[1])
            push(ps.at[k, m, after, 1], r2.at[k, m, 0, 1], k, j + R_NEAR, y_dev[0])
        if b != 1:
            push(ps.at[k, m, before, 0], r2.at[k, m, 1, 0], k, j + R_NEAR + 1, y_dev[1])

    def pass_sums(k, m, i):
        arrived(r1.at[k, m, i], k, PART * m + R_FAR + i)
        to = around(y + 1 - 2 * i)
        total = ps[k, m, to, i].astype(F32) + r1[k, m, i].astype(F32)
        ps[k, m, to, i] = total.astype(BF16)
        push(ps.at[k, m, to, i], r2.at[k, m, i, i], k, PART * m + R_SUM + i, y_dev[i])

    def activate(k):
        for m in range(2):
            for i in range(2):
                arrived(r2.at[k, m, i, 1 - i], k, PART * m + R_NEAR + i)
                arrived(r2.at[k, m, i, i], k, PART * m + R_SUM + i)
        for b in range(2):
            pre, grad = (
                ps[k, m, y, b].astype(F32)
                + r2[k, m, 0, b].astype(F32)
                + r2[k, m, 1, b].astype(F32)
                for m in range(2)
            )
            s = jax.nn.sigmoid(pre)
            hp[0, k, y, b] = (pre * s).astype(BF16)
            hp[1, k, y, b] = (grad * (s * (1.0 + pre * (1.0 - s)))).astype(BF16)
        gather_own(k, 1)

    def gather_own(k, m):
        for i in range(2):
            share(hp.at[m, k, y], k, PART * m + G_OWN + i, y_dev[i])

    def gather_far(k, m):
        for i in range(2):
            near = around(y - 1 + 2 * i)
            arrived(hp.at[m, k, near], k, PART * m + G_OWN + i)
            share(hp.at[m, k, near, i], k, PART * m + G_FWD + i, y_dev[i])

    seen = set()

    def gathered(k, m):
        if (k, m) in seen:
            return
        seen.add((k, m))
        for i in range(2):
            arrived(hp.at[m, k, around(y + 2), i], k, PART * m + G_FWD + i)

    def go_back(k):
        gathered(k, 1)

        def body(n, _):
            cols = pl.ds(pl.multiple_of(n * TILE, TILE), TILE)
            part = lax.dot_general(
                hp[1, k].reshape(NY * 2 * SLOTS, F_LOC),
                w_in[cols, :],
                (((1,), (1,)), ((), ())),
                preferred_element_type=F32,
            )
            bk[k, :, :, :, cols] = part.astype(BF16).reshape(NY, 2, SLOTS, TILE)
            return 0

        lax.fori_loop(0, D_LOC // TILE, body, 0, unroll=True)
        far, after, before = (around(y + x + d) for d in (2, 1, -1))
        for h, cols in enumerate((other, mine)):
            j = S_PART * h
            push(bk.at[k, far, 0, :, cols], q1.at[k, 0, :, cols], k, j + S_FAR, x_dev[0])
            push(bk.at[k, far, 1, :, cols], q1.at[k, 1, :, cols], k, j + S_FAR + 1, x_dev[1])
            push(bk.at[k, after, 1, :, cols], q2.at[k, 0, 1, :, cols], k, j + S_NEAR, x_dev[0])
            push(bk.at[k, before, 0, :, cols], q2.at[k, 1, 0, :, cols], k, j + S_NEAR + 1, x_dev[1])

    def back_sums(k, h):
        cols = (other, mine)[h]
        j = S_PART * h
        for i in range(2):
            arrived(q1.at[k, i, :, cols], k, j + S_FAR + i)
            to = around(y + x + 1 - 2 * i)
            total = bk[k, to, i, :, cols].astype(F32) + q1[k, i, :, cols].astype(F32)
            bk[k, to, i, :, cols] = total.astype(BF16)
            push(bk.at[k, to, i, :, cols], q2.at[k, i, i, :, cols], k, j + S_SUM + i, x_dev[i])

    def back_total(k, h):
        cols = (other, mine)[h]
        j = S_PART * h
        for i in range(2):
            arrived(q2.at[k, i, 1 - i, :, cols], k, j + S_NEAR + i)
            arrived(q2.at[k, i, i, :, cols], k, j + S_SUM + i)
        return (
            bk[k, y_from, :, :, cols].astype(F32)
            + q2[k, 0, :, :, cols].astype(F32)
            + q2[k, 1, :, :, cols].astype(F32)
        )

    def back_across(k):
        bk[k, y_from, :, :, other] = back_total(k, 0).astype(BF16)
        push(bk.at[k, y_from, :, :, other], q3.at[k], k, S_Z, z_dev)

    def send_home(k):
        arrived(q3.at[k], k, S_Z)
        rb[k] = (back_total(k, 1) + q3[k].astype(F32)).astype(BF16)
        zs = around(zh + FROM_Z[k])
        for to_core in range(2):
            push_expert(
                rb.at[k, to_core],
                ret.at[2 * k + core],
                k,
                HOME + to_core,
                zs * 2 + to_core,
                y_from,
                HOME + core,
                x == 0,
            )

    def weight_in(n):
        for k in range(NZ):
            gathered(k, 1)
        rows = pl.ds(n * TILE, TILE)
        gin[rows, :] = lax.dot_general(
            xg[0, :, :, :, :, rows].reshape(NZ * NY * 2 * SLOTS, TILE),
            hp[1].reshape(NZ * NY * 2 * SLOTS, F_LOC),
            (((0,), (0,)), ((), ())),
            preferred_element_type=F32,
        ).astype(BF16)

    def weight_out(n):
        for k in range(NZ - 1):
            gathered(k, 0)
        rows = pl.ds(n * TILE, TILE)
        acc[rows, :] = lax.dot_general(
            hp[0, : NZ - 1, :, :, :, rows].reshape((NZ - 1) * NY * 2 * SLOTS, TILE),
            xg[1, : NZ - 1].reshape((NZ - 1) * NY * 2 * SLOTS, D_LOC),
            (((0,), (0,)), ((), ())),
            preferred_element_type=F32,
        )

    def weight_out_last(n):
        gathered(NZ - 1, 0)
        rows = pl.ds(n * TILE, TILE)
        part = lax.dot_general(
            hp[0, NZ - 1, :, :, :, rows].reshape(NY * 2 * SLOTS, TILE),
            xg[1, NZ - 1].reshape(NY * 2 * SLOTS, D_LOC),
            (((0,), (0,)), ((), ())),
            preferred_element_type=F32,
        )
        gout[rows, :] = (acc[rows, :] + part).astype(BF16)

    def out_piece(dx, half, n=None):
        start = around(y - x - dx) * D_LOC + half * HALF
        rows = pl.ds(0, ing.shape[0]) if n is None else pl.ds(n * ROWS, ROWS)
        return ing.at[rows, pl.ds(pl.multiple_of(start, 128), HALF)]

    def out_copy(ref, j, dev):
        return pltpu.make_async_remote_copy(
            src_ref=ref,
            dst_ref=ref,
            send_sem=osend.at[j],
            recv_sem=orecv.at[j],
            device_id=dev,
            device_id_type=MESH,
        )

    def out_push(ref, j, dev):
        copy = out_copy(ref, j, dev)
        copy.start()
        sent.append(copy)

    def out_arrived(ref, j):
        out_copy(ref, j, z_dev).wait_recv()

    def combine():
        for k in range(NZ):
            for b in range(2):
                arrived(ret.at[2 * k + b], k, HOME + b)
        contrib = lax.dot_general(
            comb[0],
            ret[...].reshape(2 * NZ * SLOTS, HALF),
            (((0,), (0,)), ((), ())),
            preferred_element_type=F32,
        )
        start = y_to * D_LOC + c * HALF
        cols = pl.ds(pl.multiple_of(start, 128), HALF)
        ing[:, cols] = (us[:, cols].astype(F32) + contrib).astype(BF16)
        for n in range(2):
            out_push(out_piece(0, c, n), O_Z + n, z_dev)
        for i in range(2):
            out_push(out_piece(0, c), O_OWN + i, x_dev[i])

    def out_other(n):
        out_arrived(out_piece(0, 1 - c, n), O_Z + n)
        for i in range(2):
            out_push(out_piece(0, 1 - c, n), O_OTHER + 2 * n + i, x_dev[i])

    def out_right():
        out_arrived(out_piece(-1, c), O_OWN)
        out_push(out_piece(-1, c), O_FWD, x_dev[0])

    def out_left(n):
        out_arrived(out_piece(1, 1 - c, n), O_OTHER + 2 * n + 1)
        out_push(out_piece(1, 1 - c, n), O_FWD + 1 + n, x_dev[1])

    def out_end():
        out_arrived(out_piece(1, c), O_OWN + 1)
        out_arrived(out_piece(2, c), O_FWD)
        for n in range(2):
            out_arrived(out_piece(-1, 1 - c, n), O_OTHER + 2 * n)
            out_arrived(out_piece(2, 1 - c, n), O_FWD + 1 + n)

    steps = dict(
        a=share_own,
        b=share_other,
        c=pass_right,
        C=pass_left,
        d=project,
        e=pass_sums,
        f=activate,
        o=lambda k: gather_own(k, 0),
        g=lambda k: gather_far(k, 1),
        q=lambda k: gather_far(k, 0),
        h=go_back,
        i=back_sums,
        j=back_across,
        l=send_home,
        u=weight_in,
        v=weight_out,
        x=weight_out_last,
        s=start_dispatch,
        w=lambda n, *half: (combine, out_other, out_right, out_left, out_end)[n](*half),
    )
    for word in PLAN:
        steps[word[0]](*(int(n) for n in word[1:]))
    for copy in sent:
        copy.wait_send()


def store_kernel(*refs):
    *pairs, sem = refs
    copies = []
    for i in range(3):
        src, dst = pairs[i], pairs[3 + i]
        rows = src.shape[0] // 4
        for n in range(4):
            part = pl.ds(n * rows, rows)
            copies.append(pltpu.make_async_copy(src.at[part], dst.at[part], sem.at[4 * i + n]))
    for copy in copies:
        copy.start()
    for copy in copies:
        copy.wait()


def store_results(*arrays):
    hbm = pl.BlockSpec(memory_space=pl.ANY)
    size = sum(a.size * a.dtype.itemsize for a in arrays)
    return pl.pallas_call(
        store_kernel,
        out_shape=tuple(jax.ShapeDtypeStruct(a.shape, a.dtype) for a in arrays),
        in_specs=[hbm] * 3,
        out_specs=(hbm,) * 3,
        scratch_shapes=[pltpu.SemaphoreType.DMA((12,))],
        compiler_params=pltpu.CompilerParams(vmem_limit_bytes=2**20),
        cost_estimate=pl.CostEstimate(flops=0, bytes_accessed=size, transcendentals=0),
    )(*(pltpu.with_memory_space_constraint(a, pltpu.VMEM) for a in arrays))


def on_device(layer_inputs, out_grad, routes, gates, w_in, w_out):
    tokens = layer_inputs.shape[0]
    vmem = pl.BlockSpec(memory_space=pltpu.VMEM)
    hbm = pl.BlockSpec(memory_space=pl.ANY)
    rows = NY * 2 * SLOTS
    flops = 5 * 2 * NZ * rows * D_LOC * F_LOC
    in_grads, grad_in, grad_out = pl.pallas_call(
        kernel,
        out_shape=(
            pltpu.VMEM(layer_inputs.shape, BF16),
            pltpu.VMEM((D_LOC, F_LOC), BF16),
            pltpu.VMEM((F_LOC, D_LOC), BF16),
        ),
        in_specs=[hbm] * 2 + [vmem] * 2 + [hbm] * 2,
        out_specs=(vmem,) * 3,
        scratch_shapes=[
            pltpu.VMEM((2, NZ, NY, 2, SLOTS, D_LOC), BF16),
            pltpu.VMEM((NZ, 2, NY, 2, SLOTS, F_LOC), BF16),
            pltpu.VMEM((NZ, 2, 2, SLOTS, F_LOC), BF16),
            pltpu.VMEM((NZ, 2, 2, 2, SLOTS, F_LOC), BF16),
            pltpu.VMEM((2, NZ, NY, 2, SLOTS, F_LOC), BF16),
            pltpu.VMEM((NZ, NY, 2, SLOTS, D_LOC), BF16),
            pltpu.VMEM((NZ, 2, SLOTS, D_LOC), BF16),
            pltpu.VMEM((NZ, 2, 2, SLOTS, D_LOC), BF16),
            pltpu.VMEM((NZ, 2, SLOTS, HALF), BF16),
            pltpu.VMEM((NZ, 2, SLOTS, HALF), BF16),
            pltpu.VMEM((2 * NZ, SLOTS, HALF), BF16),
            pltpu.SemaphoreType.DMA((NZ + 1, COPIES)),
            pltpu.SemaphoreType.DMA((NZ + 1, COPIES)),
            pltpu.SemaphoreType.DMA((OUT_COPIES,)),
            pltpu.SemaphoreType.DMA((OUT_COPIES,)),
            pltpu.SemaphoreType.DMA((4,)),
            pltpu.VMEM((D_LOC, F_LOC), BF16),
            pltpu.VMEM((F_LOC, D_LOC), BF16),
            pltpu.VMEM((F_LOC, D_LOC), F32),
            pltpu.VMEM(layer_inputs.shape, BF16),
            pltpu.VMEM(layer_inputs.shape, BF16),
            pltpu.VMEM((2, NZ, 2, SLOTS, D_LOC), BF16),
            pltpu.VMEM((3, 2 * NZ * SLOTS, tokens), BF16),
            pltpu.VMEM((2, tokens, tokens), F32),
        ],
        compiler_params=pltpu.CompilerParams(
            collective_id=0, has_side_effects=True, vmem_limit_bytes=50 * 2**20
        ),
        cost_estimate=pl.CostEstimate(flops=flops, bytes_accessed=2**23, transcendentals=0),
    )(layer_inputs, out_grad, routes.T, gates.T, w_in[0], w_out[0])
    in_grads, grad_in, grad_out = store_results(in_grads, grad_in, grad_out)
    return (in_grads, grad_in[None], grad_out[None])


def solution(mesh):
    assert dict(mesh.shape) == {"section": 2 * NX, "expert": 2 * NZ, "dp": NY}
    return jax.shard_map(
        on_device,
        mesh=mesh,
        in_specs=(
            P(("expert", "dp"), None),
            P(("expert", "dp"), None),
            P(("expert", "dp"), None),
            P(("expert", "dp"), None),
            P("expert", "dp", "section"),
            P("expert", "section", "dp"),
        ),
        out_specs=(
            P(("expert", "dp"), None),
            P("expert", "dp", "section"),
            P("expert", "section", "dp"),
        ),
        check_vma=False,
    )
```
